128 devices in a mesh: ves: 8 (over x, core), shard: 16 (over y, z).
Axes of the slice: x: 4, y: 4, z: 4, core: 2. Of those that a mesh axis runs over, the one named last changes fastest.
Arguments:
- displacement: float32 [3, 16, 256, 128], P(None, 'ves', 'shard'), may hold values from -6 to 6
- tension: float32 [16], P('ves'), may hold values from 2 to 8
- bending: float32 [16], P('ves'), may hold values from 0.2 to 0.8
- offset: float32 [3, 16, 256, 128], P(None, 'ves', 'shard'), may hold values from 0 to 1
- owner: int32 [16, 256, 128], P('ves', 'shard'), may hold values from 0 to 127, as said below
- cell: int32 [16, 256, 128], P('ves', 'shard'), may hold values from 0 to 131071
- populations: float32 [256, 19, 256, 256], P(('ves', 'shard')), may hold values from 0 to 1, as said below
Outputs:
- membrane_force: float32 [3, 16, 256, 128], P(None, 'ves', 'shard')
- force_field: float32 [256, 3, 256, 256], P(('ves', 'shard'))
- new_populations: float32 [256, 19, 256, 256], P(('ves', 'shard'))
The draws below stay inside these ranges and needn't reach their ends.
Inputs may be any that keep to these rules, and one draw needn't show every extreme that they name: The points of one device name any one owner at most 64 times, and some owner is named exactly 64 times by the points of every device. `populations`: entries are positive.
All inputs are finite; a program needn't handle non-finite values.
Results may differ from the reference program's by a relative error of at most 0.0061.
Values sent between devices are 32-bit elements; how exact they have to be, the bound alone decides.
No kernel may reach another device: no remote copies, remote signals or barrier semaphores. Data moves between devices by JAX's collectives and lax.ppermute only.
A program may use at most 128 MiB of HBM per device.

```python
import math
import jax
import jax.numpy as jnp
from jax import lax

NXY = 256
SLAB = 2
LAT = 256
LON = 128
VES_GRP = 2
NVES = 16
NZ = 256
N_VES = 8
N_SHARD = 16


lattice_weights = [1.0 / 18, 1.0 / 36, 1.0 / 36, 1.0 / 36, 1.0 / 36, 1.0 / 18, 1.0 / 36, 1.0 / 36, 1.0 / 36, 1.0 / 36, 1.0 / 3, 1.0 / 18, 1.0 / 18, 1.0 / 18, 1.0 / 18, 1.0 / 36, 1.0 / 36, 1.0 / 36, 1.0 / 36]


def draw_populations(key, part):
    shape = (NZ, 19, NXY, NXY)
    table = jnp.array(lattice_weights, jnp.float32).reshape(1, 19, 1, 1)
    level = jax.random.uniform(key, shape, jnp.float32, 0.5, 1.5)
    return (level * table).astype(jnp.float32)


def draw_owner(key, part):
    device_count = N_VES * N_SHARD
    row_count = LAT // N_SHARD
    point_count = VES_GRP * row_count * LON
    capacity = 2 * point_count // device_count
    slot_count = device_count * capacity
    hottest = jax.random.randint(jax.random.fold_in(key, 1), (), 0, device_count)
    extra_load = jax.random.randint(jax.random.fold_in(key, 2), (device_count,), 0, 4) * 1024
    extra_load = jnp.where(jnp.arange(device_count) == hottest, 8192, extra_load)
    slot_dest = jnp.arange(slot_count, dtype=jnp.int32) // capacity

    def one_block(block_number):
        jitter = jax.random.randint(jax.random.fold_in(jax.random.fold_in(key, 3), block_number), (slot_count,), 0, 4096)
        ranking = (jitter + extra_load[slot_dest]) * slot_count + jnp.arange(slot_count, dtype=jnp.int32)
        picked_slots = jax.lax.top_k(ranking, point_count)[1]
        chosen = slot_dest[picked_slots]
        mixer = jax.random.permutation(jax.random.fold_in(jax.random.fold_in(key, 4), block_number), point_count)
        return chosen[mixer]
    blocks = jax.vmap(one_block)(jnp.arange(device_count))
    blocks = blocks.reshape(N_VES, N_SHARD, VES_GRP, row_count, LON)
    return blocks.transpose(0, 2, 1, 3, 4).reshape(N_VES * VES_GRP, LAT, LON).astype(jnp.int32)


def set_ends(entries, key, smallest, high):
    spot = [jax.random.randint(jax.random.fold_in(key, axis), (), 0, length) for axis, length in enumerate(entries.shape)]
    widest = entries.shape.index(max(entries.shape))
    beside = spot[:widest] + [(spot[widest] + 1) % entries.shape[widest]] + spot[widest + 1:]
    return entries.at[tuple(spot)].set(smallest).at[tuple(beside)].set(high)


def levels(key, extent, split, smallest, high):
    level = 1.0
    for dim, parts in split:
        draws = jax.random.uniform(jax.random.fold_in(jax.random.fold_in(key, 6), dim), (parts,), jnp.float32, smallest / len(split), high / len(split))
        level = level * jnp.repeat(jnp.exp(draws), extent[dim] // parts).reshape((-1,) + (1,) * (len(extent) - 1 - dim))
    return level


def scatter_about(stream_key, dims, deviation, limit, split=(), held_as=jnp.bfloat16):
    values = deviation * jax.random.normal(stream_key, dims, jnp.float32)
    if split:
        values = values * levels(stream_key, dims, split, -0.22, 0.18)
    return jnp.clip(values, -limit, limit).astype(held_as)


def setup_inputs(seed: int = 0) -> dict:
    seeds = jax.random.split(jax.random.key(seed), 8)
    displacement = scatter_about(seeds[0], (3, NVES, LAT, LON), 1.0, 6.0, ((1, 8), (2, 16)), jnp.float32)
    tension = jnp.clip(jnp.exp(math.log(8.0) - 1.3862944 * jax.random.uniform(seeds[1], (NVES,), jnp.float32) ** levels(seeds[1], (NVES,), ((0, 8),), -0.2, 0.2)), 2.0, 8.0)
    bending = jnp.clip(jnp.exp(math.log(0.8) - 1.3862944 * jax.random.uniform(seeds[2], (NVES,), jnp.float32) ** levels(seeds[2], (NVES,), ((0, 8),), -0.2, 0.2)), 0.2, 0.8)
    offset = jnp.clip(1.0 * jax.random.uniform(seeds[3], (3, NVES, LAT, LON), jnp.float32) ** levels(seeds[3], (3, NVES, LAT, LON), ((1, 8), (2, 16)), -0.2, 0.2), 0.0, 1.0)
    owner = draw_owner(jax.random.fold_in(seeds[7], 71), 0)
    cell = set_ends(jax.random.randint(seeds[5], (NVES, LAT, LON), 0, SLAB * NXY * NXY), jax.random.fold_in(seeds[5], 1), 0, (SLAB * NXY * NXY) - 1).astype(jnp.int32)
    populations = draw_populations(jax.random.fold_in(seeds[7], 71), 0)
    return {"displacement": displacement, "tension": tension, "bending": bending, "offset": offset, "owner": owner, "cell": cell, "populations": populations}


relax_time = 0.8
velocity_x = [0, 1, -1, 0, 0, 0, 1, -1, 0, 0, 0, 1, -1, 0, 0, 1, 1, -1, -1]
velocity_y = [0, 0, 0, 1, -1, 0, 0, 0, 1, -1, 0, 0, 0, 1, -1, 1, -1, 1, -1]
velocity_z = [1, 1, 1, 1, 1, -1, -1, -1, -1, -1, 0, 0, 0, 0, 0, 0, 0, 0, 0]
lattice_weights = [1.0 / 18, 1.0 / 36, 1.0 / 36, 1.0 / 36, 1.0 / 36, 1.0 / 18, 1.0 / 36, 1.0 / 36, 1.0 / 36, 1.0 / 36, 1.0 / 3, 1.0 / 18, 1.0 / 18, 1.0 / 18, 1.0 / 18, 1.0 / 36, 1.0 / 36, 1.0 / 36, 1.0 / 36]


def kernel_weight(distance):
    return 0.25 * (1.0 + jnp.cos(0.5 * math.pi * distance))


def surface_laplacian(field):
    padded = jnp.pad(field, ((0, 0), (0, 0), (1, 1), (0, 0)))
    center = padded[:, :, 1:-1]
    return padded[:, :, 2:] + padded[:, :, :-2] + jnp.roll(center, 1, 3) + jnp.roll(center, -1, 3) - 4.0 * center


def reference(displacement, tension, bending, offset, owner, cell, populations):
    first = surface_laplacian(displacement)
    second = surface_laplacian(first)
    membrane_force = tension[None, :, None, None] * first - bending[None, :, None, None] * second
    forces = membrane_force.reshape(3, -1)
    fraction = offset.reshape(3, -1)
    owner_flat = owner.reshape(-1).astype(jnp.int32)
    cell_flat = cell.reshape(-1).astype(jnp.int32)
    plane = cell_flat // (NXY * NXY)
    column_x = (cell_flat // NXY) % NXY
    column_y = cell_flat % NXY
    base_z = owner_flat * SLAB + plane
    coords = jnp.arange(3, dtype=jnp.int32)
    field = jnp.zeros((NZ, 3, NXY, NXY), jnp.float32)
    for reach_z in range(-1, 3):
        scaled = forces * kernel_weight(fraction[2] - reach_z)[None, :]
        plane_z = (base_z + reach_z) % NZ
        for reach_x in range(-1, 3):
            left = (scaled * kernel_weight(fraction[0] - reach_x)[None, :]).astype(jnp.bfloat16)
            left = lax.optimization_barrier(left).astype(jnp.float32)
            place_x = (column_x + reach_x) % NXY
            for reach_y in range(-1, 3):
                right = kernel_weight(fraction[1] - reach_y).astype(jnp.bfloat16)
                right = lax.optimization_barrier(right).astype(jnp.float32)
                place_y = (column_y + reach_y) % NXY
                term = left * right[None, :]
                field = field.at[plane_z[:, None], coords[None, :], place_x[:, None], place_y[:, None]].add(term.T)
    density = jnp.sum(populations, 1)
    moment_x = jnp.zeros_like(density)
    moment_y = jnp.zeros_like(density)
    moment_z = jnp.zeros_like(density)
    for item in range(19):
        moment_x = moment_x + velocity_x[item] * populations[:, item]
        moment_y = moment_y + velocity_y[item] * populations[:, item]
        moment_z = moment_z + velocity_z[item] * populations[:, item]
    flow_x = (moment_x + 0.5 * field[:, 0]) / density
    flow_y = (moment_y + 0.5 * field[:, 1]) / density
    flow_z = (moment_z + 0.5 * field[:, 2]) / density
    speed_sq = flow_x * flow_x + flow_y * flow_y + flow_z * flow_z
    moved = []
    for item in range(19):
        ex, ey, ez = velocity_x[item], velocity_y[item], velocity_z[item]
        weight = lattice_weights[item]
        along = ex * flow_x + ey * flow_y + ez * flow_z
        equilibrium = weight * density * (1.0 + 3.0 * along + 4.5 * along * along - 1.5 * speed_sq)
        push = (ex - flow_x) * field[:, 0] + (ey - flow_y) * field[:, 1] + (ez - flow_z) * field[:, 2]
        facing = ex * field[:, 0] + ey * field[:, 1] + ez * field[:, 2]
        source = weight * (3.0 * push + 9.0 * along * facing)
        current = populations[:, item]
        post = current - (current - equilibrium) / relax_time + (1.0 - 0.5 / relax_time) * source
        moved.append(jnp.roll(post, (ez, ex, ey), (0, 1, 2)))
    return membrane_force, field, jnp.stack(moved, 1)
```

```python
import functools
import math

import jax
import jax.numpy as jnp
from jax import lax
from jax.experimental import pallas as pl
from jax.experimental.pallas import tpu as pltpu
from jax.sharding import PartitionSpec as P

relax_time = 0.8
velocity_x = [0, 1, -1, 0, 0, 0, 1, -1, 0, 0, 0, 1, -1, 0, 0, 1, 1, -1, -1]
velocity_y = [0, 0, 0, 1, -1, 0, 0, 0, 1, -1, 0, 0, 0, 1, -1, 1, -1, 1, -1]
velocity_z = [1, 1, 1, 1, 1, -1, -1, -1, -1, -1, 0, 0, 0, 0, 0, 0, 0, 0, 0]
pairs = [(0, 5), (1, 7), (2, 6), (3, 9), (4, 8), (11, 12), (13, 14), (15, 18), (16, 17)]
SLOTS = 64
DEVICES = 128
WIDTH = 256
F32 = jnp.float32
BF16 = jnp.bfloat16
VMEM = pl.BlockSpec(memory_space=pltpu.VMEM)
SMEM = pl.BlockSpec(memory_space=pltpu.SMEM)
ANY = pl.BlockSpec(memory_space=pl.ANY)
LIMIT = 60 * 1024 * 1024
NT = (((1,), (1,)), ((), ()))


def iota(shape, dim):
    return lax.broadcasted_iota(jnp.int32, shape, dim)


def rank_kernel(owner_ref, cell_ref, slot_ref):
    classes = 2 * DEVICES
    before = jnp.where(iota((256, 512), 0) < iota((256, 512), 1), 1.0, 0.0)
    before = before.astype(BF16)
    label = owner_ref[...] + DEVICES * (cell_ref[...] >> 16)
    carry = jnp.zeros((classes, 256), F32)
    rows = iota((classes, 128), 0)
    for k in range(label.shape[0] // 2):
        member = jnp.concatenate(
            [jnp.where(rows == label[2 * k + s : 2 * k + s + 1], 1.0, 0.0) for s in range(2)], 1
        )
        count = jnp.dot(member.astype(BF16), before, preferred_element_type=F32)
        place = jnp.sum(member * (count[:, :256] + carry), 0, keepdims=True)
        carry = carry + count[:, 256:]
        for s in range(2):
            slot_ref[2 * k + s : 2 * k + s + 1, :] = place[:, 128 * s : 128 * s + 128].astype(
                jnp.int32
            )
    place = slot_ref[...]
    slot_ref[...] = jnp.where(label < DEVICES, place, SLOTS - 1 - place)


def pack_kernel(
    edge_ref,
    tension_ref,
    bending_ref,
    displacement_ref,
    before_ref,
    after_ref,
    offset_ref,
    owner_ref,
    cell_ref,
    slot_ref,
    force_ref,
    send_ref,
    padded_ref,
    first_ref,
    left_ref,
    right_ref,
):
    rows = displacement_ref.shape[2]
    padded_ref[:, :, 6:8] = before_ref[...]
    padded_ref[:, :, 8 : 8 + rows] = displacement_ref[...]
    padded_ref[:, :, 8 + rows : 10 + rows] = after_ref[...]

    def laplacian(ref, c, v, start, count):
        center = ref[c, v, start : start + count]
        return (
            ref[c, v, start + 1 : start + 1 + count]
            + ref[c, v, start - 1 : start - 1 + count]
            + pltpu.roll(center, 1, 1)
            + pltpu.roll(center, 127, 1)
            - 4.0 * center
        )

    for c in range(3):
        for v in range(2):
            first_ref[c, v, 8 : 8 + rows] = laplacian(padded_ref, c, v, 8, rows)
            first_ref[c, v, 7:8] = laplacian(padded_ref, c, v, 7, 1) * edge_ref[0]
            first_ref[c, v, 8 + rows : 9 + rows] = (
                laplacian(padded_ref, c, v, 8 + rows, 1) * edge_ref[1]
            )
            force_ref[c, v] = tension_ref[v] * first_ref[
                c, v, 8 : 8 + rows
            ] - bending_ref[v] * laplacian(first_ref, c, v, 8, rows)

    parts = []
    for ref in (force_ref, offset_ref):
        for c in range(3):
            value = ref[c].reshape(2 * rows, 128)
            high = value.astype(BF16).astype(F32)
            parts += [high, value - high]
    cell = cell_ref[...]
    parts += [
        ((cell >> 8) & 255).astype(F32),
        (cell & 255).astype(F32),
        (cell >> 16).astype(F32) + 1.0,
    ]
    slots = iota((SLOTS, 128), 0)
    owners = iota((DEVICES, 128), 0)
    for row in range(2 * rows):
        lanes = pl.ds(row * 128, 128)
        here = slots == slot_ref[row : row + 1]
        for n, part in enumerate(parts):
            left_ref[n * SLOTS : (n + 1) * SLOTS, lanes] = jnp.where(
                here, part[row : row + 1], 0.0
            ).astype(BF16)
        right_ref[:, lanes] = jnp.where(owners == owner_ref[row : row + 1], 1.0, 0.0).astype(BF16)
    placed = lax.dot_general(left_ref[...], right_ref[...], NT, preferred_element_type=F32)
    group = [placed[n * SLOTS : (n + 1) * SLOTS] for n in range(len(parts))]
    values = [group[2 * n] + group[2 * n + 1] for n in range(6)]
    code = jnp.where(
        group[14] > 0.5, (group[14] - 1.0) * 65536.0 + group[12] * 256.0 + group[13] + 1.0, 0.0
    )
    send_ref[...] = jnp.concatenate(values + [code], 0).T


def spread_kernel(own_ref, below_ref, above_ref, field_ref, points_ref, left_ref, right_ref):
    field_ref[...] = jnp.zeros_like(field_ref)
    group = 8
    rows16 = iota((16, 128), 0)

    def windows(base, weights):
        low = base & 15
        pieces = []
        for shift in (0, 16):
            near = rows16 + shift - low
            piece = jnp.zeros((16, 128), F32)
            for tap in range(4):
                piece = jnp.where(near == tap, weights[tap], piece)
            pieces.append(piece)
        return pieces

    for source, ref in ((0, own_ref), (-1, below_ref), (1, above_ref)):
        points_ref[...] = ref[...].T
        planes = (0, 1) if source != 1 else (1,)
        first_row = planes[0] * 768

        @pl.loop(0, SLOTS // group)
        def _(step):
            def item(n):
                return points_ref[pl.ds(pl.multiple_of(n * SLOTS + step * group, group), group), :]

            code = item(6).astype(jnp.int32)

            @pl.when(jnp.max(code) > 0)
            def _():
                cell = code - 1
                plane = cell >> 16
                base_x = (((cell >> 8) & 255) - 1) & 255
                base_y = ((cell & 255) - 1) & 255
                taps = []
                for c in range(3):
                    angle = item(3 + c) * (0.5 * math.pi)
                    cosine, sine = 0.25 * jnp.cos(angle), 0.25 * jnp.sin(angle)
                    taps.append([0.25 - sine, 0.25 + cosine, 0.25 + sine, 0.25 - cosine])
                scaled = []
                for target in planes:

                    def weight(from_plane):
                        reach = target - from_plane - 2 * source
                        return taps[2][reach + 1] if -1 <= reach <= 2 else jnp.zeros_like(code, F32)

                    weight_z = jnp.where(plane == 0, weight(0), weight(1))
                    scaled += [item(c) * weight_z for c in range(3)]
                high_x = (base_x >> 4).astype(F32)
                high_y = (base_y >> 4).astype(F32)
                for r in range(group):
                    lanes = pl.ds(r * 128, 128)

                    def at(value):
                        return jnp.broadcast_to(value[r : r + 1], (16, 128))

                    near_x = windows(at(base_x), [at(t) for t in taps[0]])
                    near_y = [p.astype(BF16) for p in windows(at(base_y), [at(t) for t in taps[1]])]
                    left = [
                        [(at(s) * piece).astype(BF16) for piece in near_x] for s in scaled
                    ]
                    block_x = at(high_x).astype(BF16)
                    block_y = at(high_y).astype(BF16)
                    zero = jnp.zeros((16, 128), BF16)
                    for g in range(16):
                        is_y = block_y == jnp.asarray(g, BF16)
                        was_y = block_y == jnp.asarray((g - 1) % 16, BF16)
                        right_ref[16 * g : 16 * g + 16, lanes] = jnp.where(
                            is_y, near_y[0], jnp.where(was_y, near_y[1], zero)
                        )
                        is_x = block_x == jnp.asarray(g, BF16)
                        was_x = block_x == jnp.asarray((g - 1) % 16, BF16)
                        for n, (low, high) in enumerate(left):
                            left_ref[pl.ds(256 * n + 16 * g, 16), lanes] = jnp.where(
                                is_x, low, jnp.where(was_x, high, zero)
                            )
                count = 768 * len(planes)
                field_ref[first_row : first_row + count] += lax.dot_general(
                    left_ref[0:count], right_ref[...], NT, preferred_element_type=F32
                )


def signed(item, vector):
    total = None
    for sign, value in zip((velocity_x[item], velocity_y[item], velocity_z[item]), vector):
        if sign:
            value = value if sign > 0 else -value
            total = value if total is None else total + value
    return total


def post_collision(current, push):
    density = current[0]
    for item in range(1, 19):
        density = density + current[item]
    moment = []
    for table in (velocity_x, velocity_y, velocity_z):
        plus = [current[i] for i in range(19) if table[i] > 0]
        minus = [current[i] for i in range(19) if table[i] < 0]
        moment.append(functools.reduce(jnp.add, plus) - functools.reduce(jnp.add, minus))
    inverse = 1.0 / density
    rate = 1.0 / relax_time
    half = 1.0 - 0.5 * rate
    flux = [m + 0.5 * f for m, f in zip(moment, push)]
    flow = [j * inverse for j in flux]
    rest = rate * density
    for u, j, f in zip(flow, flux, push):
        rest = rest - u * ((1.5 * rate) * j + (3.0 * half) * f)
    linear = [(3.0 * rate) * j + (3.0 * half) * f for j, f in zip(flux, push)]
    square = [(4.5 * rate) * j + (9.0 * half) * f for j, f in zip(flux, push)]
    result = [None] * 19
    result[10] = (1.0 - rate) * current[10] + (1.0 / 3) * rest
    for one, other in pairs:
        weight = 1.0 / 18 if one in (0, 11, 13) else 1.0 / 36
        even = weight * (rest + signed(one, flow) * signed(one, square))
        odd = weight * signed(one, linear)
        result[one] = (1.0 - rate) * current[one] + (even + odd)
        result[other] = (1.0 - rate) * current[other] + (even - odd)
    return result


def collide_kernel(
    populations_ref, field_ref, moved_ref, up_ref, down_ref, in_ref, out_ref, carry_ref, in_sem, out_sem
):
    loads = [pltpu.make_async_copy(populations_ref.at[z], in_ref.at[z], in_sem.at[z]) for z in range(2)]
    for copy in loads:
        copy.start()
    stores = []
    row = iota((8, WIDTH), 0)
    for z in range(2):
        loads[z].wait()

        @pl.loop(0, 34)
        def _(step):
            now = pl.multiple_of(((step + 31) & 31) * 8, 8)
            last = pl.multiple_of(((step + 30) & 31) * 8, 8)
            current = [in_ref[z, i, pl.ds(now, 8), :] for i in range(19)]
            push = [field_ref[z, c, pl.ds(now, 8), :] for c in range(3)]
            result = post_collision(current, push)
            slot = 0
            for i in range(19):
                value = result[i]
                if velocity_y[i]:
                    value = pltpu.roll(value, velocity_y[i] % WIDTH, 1)
                if velocity_x[i] == 0:
                    out_ref[z, i, pl.ds(now, 8), :] = value
                    continue
                value = pltpu.roll(value, velocity_x[i] % 8, 0)
                old = carry_ref[slot]
                carry_ref[slot] = value
                slot += 1
                if velocity_x[i] > 0:
                    out_ref[z, i, pl.ds(now, 8), :] = jnp.where(row == 0, old, value)
                else:
                    out_ref[z, i, pl.ds(last, 8), :] = jnp.where(row == 7, value, old)

        for n, (start, stop, place) in enumerate(
            (
                (0, 5, moved_ref.at[1, 0:5] if z == 0 else up_ref),
                (5, 10, moved_ref.at[0, 5:10] if z == 1 else down_ref),
                (10, 19, moved_ref.at[z, 10:19]),
            )
        ):
            copy = pltpu.make_async_copy(out_ref.at[z, start:stop], place, out_sem.at[z, n])
            copy.start()
            stores.append(copy)
    for copy in stores:
        copy.wait()


def place_kernel(up_ref, down_ref, held_ref, moved_ref, sem):
    copies = [
        pltpu.make_async_copy(up_ref, moved_ref.at[0, 0:5], sem.at[0]),
        pltpu.make_async_copy(down_ref, moved_ref.at[1, 5:10], sem.at[1]),
    ]
    for copy in copies:
        copy.start()
    for copy in copies:
        copy.wait()


def passed_along(value, steps, axis=("ves", "shard"), wrap=True):
    count = math.prod(lax.axis_size(a) for a in axis)
    return lax.ppermute(
        value,
        axis,
        [(i, (i + steps) % count) for i in range(count) if wrap or 0 <= i + steps < count],
    )


def params():
    return pltpu.CompilerParams(vmem_limit_bytes=LIMIT)


def on_device(displacement, tension, bending, offset, owner, cell, populations):
    shape = jax.ShapeDtypeStruct
    before = passed_along(displacement[:, :, -2:], 1, ("shard",), False)
    after = passed_along(displacement[:, :, :2], -1, ("shard",), False)
    owner_rows = owner.reshape(32, 128)
    cell_rows = cell.reshape(32, 128)
    slot = pl.pallas_call(
        rank_kernel,
        out_shape=shape((32, 128), jnp.int32),
        in_specs=[VMEM] * 2,
        out_specs=VMEM,
        compiler_params=params(),
        name="rank",
    )(owner_rows, cell_rows)
    here = lax.axis_index("shard")
    edge = jnp.stack([here > 0, here < lax.axis_size("shard") - 1]).astype(F32)
    membrane_force, send = pl.pallas_call(
        pack_kernel,
        out_shape=(shape((3, 2, 16, 128), F32), shape((DEVICES, 7 * SLOTS), F32)),
        in_specs=[SMEM] * 3 + [VMEM] * 7,
        out_specs=(VMEM, VMEM),
        scratch_shapes=[
            pltpu.VMEM((3, 2, 32, 128), F32),
            pltpu.VMEM((3, 2, 32, 128), F32),
            pltpu.VMEM((15 * SLOTS, 4096), BF16),
            pltpu.VMEM((DEVICES, 4096), BF16),
        ],
        compiler_params=params(),
        name="pack",
    )(
        edge, tension, bending, displacement, before, after, offset, owner_rows, cell_rows, slot
    )
    own = lax.all_to_all(send, ("ves", "shard"), split_axis=0, concat_axis=0, tiled=True)
    below = passed_along(own, 1)
    above = passed_along(own, -1)
    field = pl.pallas_call(
        spread_kernel,
        out_shape=shape((1536, WIDTH), F32),
        in_specs=[VMEM] * 3,
        out_specs=VMEM,
        scratch_shapes=[
            pltpu.VMEM((7 * SLOTS, 128), F32),
            pltpu.VMEM((1536, 1024), BF16),
            pltpu.VMEM((256, 1024), BF16),
        ],
        compiler_params=params(),
        name="spread",
    )(own, below, above)
    force_field = field.reshape(2, 3, WIDTH, WIDTH)
    moved, up, down = pl.pallas_call(
        collide_kernel,
        out_shape=(
            shape((2, 19, WIDTH, WIDTH), F32),
            shape((5, WIDTH, WIDTH), F32),
            shape((5, WIDTH, WIDTH), F32),
        ),
        in_specs=[ANY, VMEM],
        out_specs=(ANY, ANY, ANY),
        scratch_shapes=[
            pltpu.VMEM((2, 19, WIDTH, WIDTH), F32),
            pltpu.VMEM((2, 19, WIDTH, WIDTH), F32),
            pltpu.VMEM((10, 8, WIDTH), F32),
            pltpu.SemaphoreType.DMA((2,)),
            pltpu.SemaphoreType.DMA((2, 3)),
        ],
        compiler_params=params(),
        name="collide",
    )(populations, force_field)
    up = passed_along(up, 1)
    down = passed_along(down, -1)
    moved = pl.pallas_call(
        place_kernel,
        out_shape=shape((2, 19, WIDTH, WIDTH), F32),
        in_specs=[VMEM, VMEM, ANY],
        out_specs=ANY,
        scratch_shapes=[pltpu.SemaphoreType.DMA((2,))],
        input_output_aliases={2: 0},
        compiler_params=params(),
        name="place",
    )(up, down, moved)
    return (membrane_force, force_field, moved)


def solution(mesh):
    return jax.shard_map(
        on_device,
        mesh=mesh,
        in_specs=(
            P(None, "ves", "shard", None),
            P("ves"),
            P("ves"),
            P(None, "ves", "shard", None),
            P("ves", "shard", None),
            P("ves", "shard", None),
            P(("ves", "shard"), None, None, None),
        ),
        out_specs=(
            P(None, "ves", "shard", None),
            P(("ves", "shard"), None, None, None),
            P(("ves", "shard"), None, None, None),
        ),
        check_vma=False,
    )
```

```python
import functools
import math

import jax
import jax.numpy as jnp
from jax import lax
from jax.experimental import pallas as pl
from jax.experimental.pallas import tpu as pltpu
from jax.sharding import PartitionSpec as P

relax_time = 0.8
velocity_x = [0, 1, -1, 0, 0, 0, 1, -1, 0, 0, 0, 1, -1, 0, 0, 1, 1, -1, -1]
velocity_y = [0, 0, 0, 1, -1, 0, 0, 0, 1, -1, 0, 0, 0, 1, -1, 1, -1, 1, -1]
velocity_z = [1, 1, 1, 1, 1, -1, -1, -1, -1, -1, 0, 0, 0, 0, 0, 0, 0, 0, 0]
pairs = [(0, 5), (1, 7), (2, 6), (3, 9), (4, 8), (11, 12), (13, 14), (15, 18), (16, 17)]
SLOTS = 64
DEVICES = 128
WIDTH = 256
F32 = jnp.float32
BF16 = jnp.bfloat16
VMEM = pl.BlockSpec(memory_space=pltpu.VMEM)
SMEM = pl.BlockSpec(memory_space=pltpu.SMEM)
ANY = pl.BlockSpec(memory_space=pl.ANY)
CHUNKS = (64, 64, 64, 64)
NT = (((1,), (1,)), ((), ()))


def iota(shape, dim):
    return lax.broadcasted_iota(jnp.int32, shape, dim)


def rank_kernel(owner_ref, cell_ref, slot_ref):
    classes = 2 * DEVICES
    before = jnp.where(iota((256, 512), 0) < iota((256, 512), 1), 1.0, 0.0)
    before = before.astype(BF16)
    label = owner_ref[...] + DEVICES * (cell_ref[...] >> 16)
    carry = jnp.zeros((classes, 256), F32)
    rows = iota((classes, 128), 0)
    for k in range(label.shape[0] // 2):
        member = jnp.concatenate(
            [jnp.where(rows == label[2 * k + s : 2 * k + s + 1], 1.0, 0.0) for s in range(2)], 1
        )
        count = jnp.dot(member.astype(BF16), before, preferred_element_type=F32)
        place = jnp.sum(member * (count[:, :256] + carry), 0, keepdims=True)
        carry = carry + count[:, 256:]
        for s in range(2):
            slot_ref[2 * k + s : 2 * k + s + 1, :] = place[:, 128 * s : 128 * s + 128].astype(
                jnp.int32
            )
    place = slot_ref[...]
    slot_ref[...] = jnp.where(label < DEVICES, place, SLOTS - 1 - place)


def pack_kernel(
    tension_ref,
    bending_ref,
    displacement_ref,
    before_ref,
    after_ref,
    offset_ref,
    owner_ref,
    cell_ref,
    slot_ref,
    force_ref,
    send_ref,
    padded_ref,
    first_ref,
    left_ref,
    right_ref,
):
    rows = displacement_ref.shape[2]
    here = lax.axis_index("shard")
    inside = ((here > 0).astype(F32), (here < lax.axis_size("shard") - 1).astype(F32))
    padded_ref[:, :, 6:8] = before_ref[...]
    padded_ref[:, :, 8 : 8 + rows] = displacement_ref[...]
    padded_ref[:, :, 8 + rows : 10 + rows] = after_ref[...]

    def laplacian(ref, c, v, start, count):
        center = ref[c, v, start : start + count]
        return (
            ref[c, v, start + 1 : start + 1 + count]
            + ref[c, v, start - 1 : start - 1 + count]
            + pltpu.roll(center, 1, 1)
            + pltpu.roll(center, 127, 1)
            - 4.0 * center
        )

    for c in range(3):
        for v in range(2):
            first_ref[c, v, 8 : 8 + rows] = laplacian(padded_ref, c, v, 8, rows)
            first_ref[c, v, 7:8] = laplacian(padded_ref, c, v, 7, 1) * inside[0]
            first_ref[c, v, 8 + rows : 9 + rows] = (
                laplacian(padded_ref, c, v, 8 + rows, 1) * inside[1]
            )
            force_ref[c, v] = tension_ref[v] * first_ref[
                c, v, 8 : 8 + rows
            ] - bending_ref[v] * laplacian(first_ref, c, v, 8, rows)

    parts = []
    for ref in (force_ref, offset_ref):
        for c in range(3):
            value = ref[c].reshape(2 * rows, 128)
            high = value.astype(BF16).astype(F32)
            parts += [high, value - high]
    cell = cell_ref[...]
    parts += [
        ((cell >> 8) & 255).astype(F32),
        (cell & 255).astype(F32),
        (cell >> 16).astype(F32) + 1.0,
    ]
    slots = iota((SLOTS, 128), 0)
    owners = iota((DEVICES, 128), 0)
    for row in range(2 * rows):
        lanes = pl.ds(row * 128, 128)
        here = slots == slot_ref[row : row + 1]
        for n, part in enumerate(parts):
            left_ref[n * SLOTS : (n + 1) * SLOTS, lanes] = jnp.where(
                here, part[row : row + 1], 0.0
            ).astype(BF16)
        right_ref[:, lanes] = jnp.where(owners == owner_ref[row : row + 1], 1.0, 0.0).astype(BF16)
    placed = lax.dot_general(left_ref[...], right_ref[...], NT, preferred_element_type=F32)
    group = [placed[n * SLOTS : (n + 1) * SLOTS] for n in range(len(parts))]
    values = [group[2 * n] + group[2 * n + 1] for n in range(6)]
    code = jnp.where(
        group[14] > 0.5, (group[14] - 1.0) * 65536.0 + group[12] * 256.0 + group[13] + 1.0, 0.0
    )
    send_ref[:, 0, :] = jnp.concatenate(values + [code], 0).T


GROUP = 8


def spread_source(points_ref, source, targets, listed_ref, total, buffers, add):
    rows16 = iota((16, 128), 0)

    def windows(base, weights):
        low = base & 15
        pieces = []
        for shift in (0, 16):
            near = rows16 + shift - low
            piece = jnp.zeros((16, 128), F32)
            for tap in range(4):
                piece = jnp.where(near == tap, weights[tap], piece)
            pieces.append(piece)
        return pieces

    def build(index, left_ref, right_ref):
        step = listed_ref[jnp.minimum(index, total)]
        used = (index < total).astype(F32)

        def item(n):
            return points_ref[pl.ds(pl.multiple_of(n * SLOTS + step * GROUP, GROUP), GROUP), :]

        cell = item(6).astype(jnp.int32) - 1
        plane = cell >> 16
        base_x = (((cell >> 8) & 255) - 1) & 255
        base_y = ((cell & 255) - 1) & 255
        taps = []
        for c in range(3):
            angle = item(3 + c) * (0.5 * math.pi)
            cosine, sine = 0.25 * jnp.cos(angle), 0.25 * jnp.sin(angle)
            taps.append([0.25 - sine, 0.25 + cosine, 0.25 + sine, 0.25 - cosine])
        scaled = []
        for target in targets:

            def weight(from_plane):
                reach = target - from_plane - 2 * source
                return taps[2][reach + 1] if -1 <= reach <= 2 else jnp.zeros((GROUP, 128), F32)

            weight_z = jnp.where(plane == 0, weight(0), weight(1)) * used
            scaled += [item(c) * weight_z for c in range(3)]
        high_x = (base_x >> 4).astype(F32)
        high_y = (base_y >> 4).astype(F32)
        zero = jnp.zeros((16, 128), BF16)

        def slice_of(r):
            lanes = pl.ds(r * 128, 128)

            def at(value):
                return jnp.broadcast_to(value[r : r + 1], (16, 128))

            near_x = windows(at(base_x), [at(t) for t in taps[0]])
            near_y = [p.astype(BF16) for p in windows(at(base_y), [at(t) for t in taps[1]])]
            left = [[(at(s) * piece).astype(BF16) for piece in near_x] for s in scaled]
            block_x = at(high_x).astype(BF16)
            block_y = at(high_y).astype(BF16)
            is_x = [block_x == jnp.asarray(g, BF16) for g in range(16)]
            is_y = [block_y == jnp.asarray(g, BF16) for g in range(16)]
            for g in range(16):
                right_ref[16 * g : 16 * g + 16, lanes] = jnp.where(
                    is_y[g], near_y[0], jnp.where(is_y[g - 1], near_y[1], zero)
                )
                for n, (low, high) in enumerate(left):
                    left_ref[pl.ds(256 * n + 16 * g, 16), lanes] = jnp.where(
                        is_x[g], low, jnp.where(is_x[g - 1], high, zero)
                    )

        return slice_of

    rows = 768 * len(targets)
    first = targets[0] * 768

    def product(left_ref, right_ref, n):
        add(
            first + 256 * n,
            256,
            lax.dot_general(
                left_ref[256 * n : 256 * n + 256], right_ref[...], NT, preferred_element_type=F32
            ),
        )

    (left_0, right_0), (left_1, right_1) = buffers
    parts = 3 * len(targets)

    def both(left_a, right_a, index, left_b, right_b):
        slice_of = build(index, left_b, right_b)
        done = 0
        for n in range(parts):
            product(left_a, right_a, n)
            while done * parts < (n + 1) * GROUP and done < GROUP:
                slice_of(done)
                done += 1

    @pl.when(total > 0)
    def _():
        slice_of = build(0, left_0, right_0)
        for r in range(GROUP):
            slice_of(r)

        @pl.loop(0, (total + 1) >> 1)
        def _(turn):
            both(left_0, right_0, 2 * turn + 1, left_1, right_1)
            both(left_1, right_1, 2 * turn + 2, left_0, right_0)


def listed(points_ref, listed_ref, wanted):
    total = jnp.int32(0)
    for step in range(SLOTS // GROUP):
        start = 6 * SLOTS + step * GROUP
        found = wanted(points_ref[start : start + GROUP, :])
        listed_ref[total] = step
        total = total + found.astype(jnp.int32)
    listed_ref[total] = 0
    return total


def has_plane_0(code):
    return jnp.max(jnp.where((code > 0.5) & (code < 65536.5), 1.0, 0.0)) > 0.5


def has_plane_1(code):
    return jnp.max(code) > 65536.5


def only_plane_0(code):
    most = jnp.max(code)
    return (most > 0.5) & (most < 65536.5)


def spread_own_kernel(own_ref, field_ref, points_ref, left_0, right_0, left_1, right_1, list_ref):
    points_ref[...] = own_ref[...].T
    field_ref[...] = jnp.zeros_like(field_ref)

    def add(first, rows, value):
        field_ref[first : first + rows] += value

    buffers = ((left_0, right_0), (left_1, right_1))
    total = listed(points_ref, list_ref, lambda code: jnp.max(code) > 0.5)
    spread_source(points_ref, 0, (0, 1), list_ref, total, buffers, add)


def spread_near_kernel(
    below_ref, above_ref, held_ref, field_ref, points_ref, left_0, right_0, left_1, right_1, list_ref
):
    def add(first, rows, value):
        field_ref[first : first + rows] += value

    buffers = ((left_0, right_0), (left_1, right_1))
    field_ref[...] = held_ref[...]
    points_ref[...] = below_ref[...].T
    total = listed(points_ref, list_ref, has_plane_1)
    spread_source(points_ref, -1, (0, 1), list_ref, total, buffers, add)
    total = listed(points_ref, list_ref, only_plane_0)
    spread_source(points_ref, -1, (0,), list_ref, total, buffers, add)
    points_ref[...] = above_ref[...].T
    total = listed(points_ref, list_ref, has_plane_0)
    spread_source(points_ref, 1, (1,), list_ref, total, buffers, add)


def spread_own(own):
    return pl.pallas_call(
        spread_own_kernel,
        out_shape=jax.ShapeDtypeStruct((1536, WIDTH), F32),
        in_specs=[VMEM],
        out_specs=VMEM,
        scratch_shapes=spread_scratch(),
        compiler_params=params(14),
        name="spread_own",
    )(own)


def spread_near(below, above, field):
    return pl.pallas_call(
        spread_near_kernel,
        out_shape=jax.ShapeDtypeStruct((1536, WIDTH), F32),
        in_specs=[VMEM] * 3,
        out_specs=VMEM,
        scratch_shapes=spread_scratch(),
        compiler_params=params(16),
        name="spread_near",
    )(below, above, field)


def spread_scratch():
    return [pltpu.VMEM((7 * SLOTS, 128), F32)] + [
        pltpu.VMEM((1536, 128 * GROUP), BF16),
        pltpu.VMEM((256, 128 * GROUP), BF16),
    ] * 2 + [pltpu.SMEM((SLOTS // GROUP + 1,), jnp.int32)]


def signed(item, vector):
    total = None
    for sign, value in zip((velocity_x[item], velocity_y[item], velocity_z[item]), vector):
        if sign:
            value = value if sign > 0 else -value
            total = value if total is None else total + value
    return total


def post_collision(current, push):
    density = current[0]
    for item in range(1, 19):
        density = density + current[item]
    moment = []
    for table in (velocity_x, velocity_y, velocity_z):
        plus = [current[i] for i in range(19) if table[i] > 0]
        minus = [current[i] for i in range(19) if table[i] < 0]
        moment.append(functools.reduce(jnp.add, plus) - functools.reduce(jnp.add, minus))
    inverse = 1.0 / density
    rate = 1.0 / relax_time
    half = 1.0 - 0.5 * rate
    flux = [m + 0.5 * f for m, f in zip(moment, push)]
    flow = [j * inverse for j in flux]
    rest = rate * density
    for u, j, f in zip(flow, flux, push):
        rest = rest - u * ((1.5 * rate) * j + (3.0 * half) * f)
    linear = [(3.0 * rate) * j + (3.0 * half) * f for j, f in zip(flux, push)]
    square = [(4.5 * rate) * j + (9.0 * half) * f for j, f in zip(flux, push)]
    result = [None] * 19
    result[10] = (1.0 - rate) * current[10] + (1.0 / 3) * rest
    for one, other in pairs:
        weight = 1.0 / 18 if one in (0, 11, 13) else 1.0 / 36
        even = weight * (rest + signed(one, flow) * signed(one, square))
        odd = weight * signed(one, linear)
        result[one] = (1.0 - rate) * current[one] + (even + odd)
        result[other] = (1.0 - rate) * current[other] + (even - odd)
    return result


def collide_kernel(start, rows, populations_ref, field_ref, held_ref, moved_ref, up_ref, down_ref, in_ref, out_ref, carry_ref, in_sem, out_sem):
    spans = [(start - 8, rows + 16, 0)]
    if start == 0:
        spans = [(WIDTH - 8, 8, 0), (0, rows + 8, 8)]
    elif start + rows == WIDTH:
        spans = [(start - 8, rows + 8, 0), (0, 8, rows + 8)]
    loads = [
        [
            pltpu.make_async_copy(
                populations_ref.at[z, :, pl.ds(first, count)],
                in_ref.at[z, :, pl.ds(place, count)],
                in_sem.at[z, n],
            )
            for n, (first, count, place) in enumerate(spans)
        ]
        for z in range(2)
    ]
    for copy in loads[0] + loads[1]:
        copy.start()
    stores = []
    row = iota((8, WIDTH), 0)
    for z in range(2):
        for copy in loads[z]:
            copy.wait()

        @pl.loop(0, rows // 8 + 2, unroll=5)
        def _(step):
            here = pl.multiple_of(step * 8, 8)
            now = pl.multiple_of(step * 8 + 8, 8)
            field_row = pl.multiple_of((start - 8 + WIDTH + step * 8) & (WIDTH - 1), 8)
            current = [in_ref[z, i, pl.ds(here, 8), :] for i in range(19)]
            push = [field_ref[z, c, pl.ds(field_row, 8), :] for c in range(3)]
            result = post_collision(current, push)
            slot = 0
            for i in range(19):
                value = result[i]
                if velocity_y[i]:
                    value = pltpu.roll(value, velocity_y[i] % WIDTH, 1)
                if velocity_x[i] == 0:
                    out_ref[z, i, pl.ds(now, 8), :] = value
                    continue
                value = pltpu.roll(value, velocity_x[i] % 8, 0)
                old = carry_ref[slot]
                carry_ref[slot] = value
                slot += 1
                if velocity_x[i] > 0:
                    out_ref[z, i, pl.ds(now, 8), :] = jnp.where(row == 0, old, value)
                else:
                    out_ref[z, i, pl.ds(here, 8), :] = jnp.where(row == 7, value, old)

        within = pl.ds(start, rows)
        for n, (low, high, place) in enumerate(
            (
                (0, 5, moved_ref.at[1, 0:5, within] if z == 0 else up_ref),
                (5, 10, moved_ref.at[0, 5:10, within] if z == 1 else down_ref),
                (10, 19, moved_ref.at[z, 10:19, within]),
            )
        ):
            copy = pltpu.make_async_copy(
                out_ref.at[z, low:high, pl.ds(16, rows)], place, out_sem.at[z, n]
            )
            copy.start()
            stores.append(copy)
    for copy in stores:
        copy.wait()


def collide(start, rows, populations, field, held):
    shape = jax.ShapeDtypeStruct
    return pl.pallas_call(
        functools.partial(collide_kernel, start, rows),
        out_shape=(
            shape((2, 19, WIDTH, WIDTH), F32),
            shape((5, rows, WIDTH), F32),
            shape((5, rows, WIDTH), F32),
        ),
        in_specs=[ANY, VMEM, ANY],
        out_specs=(ANY, ANY, ANY),
        scratch_shapes=[
            pltpu.VMEM((2, 19, rows + 16, WIDTH), F32),
            pltpu.VMEM((2, 19, rows + 24, WIDTH), F32),
            pltpu.VMEM((10, 8, WIDTH), F32),
            pltpu.SemaphoreType.DMA((2, 2)),
            pltpu.SemaphoreType.DMA((2, 3)),
        ],
        input_output_aliases={2: 0} if held.shape[0] == 2 else {},
        compiler_params=params(14),
        name="collide",
    )(populations, field, held)


def place_kernel(starts, *refs):
    count = len(starts)
    ups, downs = refs[:count], refs[count : 2 * count]
    moved_ref, sem = refs[2 * count + 1 :]
    copies = []
    for n, start in enumerate(starts):
        within = pl.ds(start, ups[n].shape[1])
        copies += [
            pltpu.make_async_copy(ups[n], moved_ref.at[0, 0:5, within], sem.at[0, n]),
            pltpu.make_async_copy(downs[n], moved_ref.at[1, 5:10, within], sem.at[1, n]),
        ]
    for copy in copies:
        copy.start()
    for copy in copies:
        copy.wait()


def place(starts, ups, downs, moved):
    count = len(starts)
    return pl.pallas_call(
        functools.partial(place_kernel, starts),
        out_shape=jax.ShapeDtypeStruct(moved.shape, F32),
        in_specs=[VMEM] * (2 * count) + [ANY],
        out_specs=ANY,
        scratch_shapes=[pltpu.SemaphoreType.DMA((2, count))],
        input_output_aliases={2 * count: 0},
        compiler_params=params(8),
        name="place",
    )(*ups, *downs, moved)


def passed_along(value, steps, axis=("ves", "shard"), wrap=True):
    count = math.prod(lax.axis_size(a) for a in axis)
    return lax.ppermute(
        value,
        axis,
        [(i, (i + steps) % count) for i in range(count) if wrap or 0 <= i + steps < count],
    )


def params(megabytes):
    return pltpu.CompilerParams(vmem_limit_bytes=megabytes * 1024 * 1024)


def on_device(displacement, tension, bending, offset, owner, cell, populations):
    shape = jax.ShapeDtypeStruct
    before = passed_along(displacement[:, :, -2:], 1, ("shard",), False)
    after = passed_along(displacement[:, :, :2], -1, ("shard",), False)
    owner_rows = owner.reshape(32, 128)
    cell_rows = cell.reshape(32, 128)
    slot = pl.pallas_call(
        rank_kernel,
        out_shape=shape((32, 128), jnp.int32),
        in_specs=[VMEM] * 2,
        out_specs=VMEM,
        compiler_params=params(6),
        name="rank",
    )(owner_rows, cell_rows)
    membrane_force, send = pl.pallas_call(
        pack_kernel,
        out_shape=(shape((3, 2, 16, 128), F32), shape((DEVICES, 1, 7 * SLOTS), F32)),
        in_specs=[SMEM] * 2 + [VMEM] * 7,
        out_specs=(VMEM, VMEM),
        scratch_shapes=[
            pltpu.VMEM((3, 2, 32, 128), F32),
            pltpu.VMEM((3, 2, 32, 128), F32),
            pltpu.VMEM((15 * SLOTS, 4096), BF16),
            pltpu.VMEM((DEVICES, 4096), BF16),
        ],
        compiler_params=params(20),
        name="pack",
    )(
        tension, bending, displacement, before, after, offset, owner_rows, cell_rows, slot
    )
    own = lax.all_to_all(send, ("ves", "shard"), split_axis=0, concat_axis=0, tiled=True)
    own = own.reshape(DEVICES, 7 * SLOTS)
    below = passed_along(own, 1)
    above = passed_along(own, -1)
    field = spread_near(below, above, spread_own(own))
    force_field = field.reshape(2, 3, WIDTH, WIDTH)
    moved = jnp.zeros((1, 8, 128), F32)
    ups, downs, starts = [], [], []
    start = 0
    for rows in CHUNKS:
        moved, up, down = collide(start, rows, populations, force_field, moved)
        ups.append(passed_along(up, 1))
        downs.append(passed_along(down, -1))
        starts.append(start)
        start += rows
    moved = place(starts[:-1], ups[:-1], downs[:-1], moved)
    moved = place(starts[-1:], ups[-1:], downs[-1:], moved)
    return (membrane_force, force_field, moved)


def solution(mesh):
    return jax.shard_map(
        on_device,
        mesh=mesh,
        in_specs=(
            P(None, "ves", "shard", None),
            P("ves"),
            P("ves"),
            P(None, "ves", "shard", None),
            P("ves", "shard", None),
            P("ves", "shard", None),
            P(("ves", "shard"), None, None, None),
        ),
        out_specs=(
            P(None, "ves", "shard", None),
            P(("ves", "shard"), None, None, None),
            P(("ves", "shard"), None, None, None),
        ),
        check_vma=False,
    )
```

```python
import functools
import math

import jax
import jax.numpy as jnp
from jax import lax
from jax.experimental import pallas as pl
from jax.experimental.pallas import tpu as pltpu
from jax.sharding import PartitionSpec as P

relax_time = 0.8
velocity_x = [0, 1, -1, 0, 0, 0, 1, -1, 0, 0, 0, 1, -1, 0, 0, 1, 1, -1, -1]
velocity_y = [0, 0, 0, 1, -1, 0, 0, 0, 1, -1, 0, 0, 0, 1, -1, 1, -1, 1, -1]
velocity_z = [1, 1, 1, 1, 1, -1, -1, -1, -1, -1, 0, 0, 0, 0, 0, 0, 0, 0, 0]
pairs = [(0, 5), (1, 7), (2, 6), (3, 9), (4, 8), (11, 12), (13, 14), (15, 18), (16, 17)]
SLOTS = 64
DEVICES = 128
WIDTH = 256
F32 = jnp.float32
BF16 = jnp.bfloat16
VMEM = pl.BlockSpec(memory_space=pltpu.VMEM)
SMEM = pl.BlockSpec(memory_space=pltpu.SMEM)
ANY = pl.BlockSpec(memory_space=pl.ANY)
HBM = pl.BlockSpec(memory_space=pltpu.HBM)
CHUNKS = (128, 128)
NT = (((1,), (1,)), ((), ()))


def iota(shape, dim):
    return lax.broadcasted_iota(jnp.int32, shape, dim)


def fetch(moves, sem):
    copies = [pltpu.make_async_copy(*move, sem.at[n]) for n, move in enumerate(moves)]
    for copy in copies:
        copy.start()
    for copy in copies:
        copy.wait()


def rank_kernel(owner_from, cell_from, slot_ref, owner_ref, cell_ref, sem):
    fetch(((owner_from, owner_ref), (cell_from, cell_ref)), sem)
    classes = 2 * DEVICES
    before = jnp.where(iota((256, 512), 0) < iota((256, 512), 1), 1.0, 0.0)
    before = before.astype(BF16)
    label = owner_ref[...] + DEVICES * (cell_ref[...] >> 16)
    carry = jnp.zeros((classes, 256), F32)
    rows = iota((classes, 128), 0)
    for k in range(label.shape[0] // 2):
        member = jnp.concatenate(
            [jnp.where(rows == label[2 * k + s : 2 * k + s + 1], 1.0, 0.0) for s in range(2)], 1
        )
        count = jnp.dot(member.astype(BF16), before, preferred_element_type=F32)
        place = jnp.sum(member * (count[:, :256] + carry), 0, keepdims=True)
        carry = carry + count[:, 256:]
        for s in range(2):
            slot_ref[2 * k + s : 2 * k + s + 1, :] = place[:, 128 * s : 128 * s + 128].astype(
                jnp.int32
            )
    place = slot_ref[...]
    slot_ref[...] = jnp.where(label < DEVICES, place, SLOTS - 1 - place)


def pack_kernel(
    tension_from,
    bending_from,
    displacement_from,
    before_ref,
    after_ref,
    offset_from,
    owner_from,
    cell_from,
    slot_ref,
    force_ref,
    send_ref,
    tension_ref,
    bending_ref,
    offset_ref,
    owner_ref,
    cell_ref,
    padded_ref,
    first_ref,
    left_ref,
    right_ref,
    sem,
):
    rows = displacement_from.shape[2]
    fetch(
        (
            (tension_from, tension_ref),
            (bending_from, bending_ref),
            (offset_from, offset_ref),
            (owner_from, owner_ref),
            (cell_from, cell_ref),
            (displacement_from, padded_ref.at[:, :, pl.ds(8, rows)]),
        ),
        sem,
    )
    here = lax.axis_index("shard")
    inside = ((here > 0).astype(F32), (here < lax.axis_size("shard") - 1).astype(F32))
    padded_ref[:, :, 6:8] = before_ref[...]
    padded_ref[:, :, 8 + rows : 10 + rows] = after_ref[...]

    def laplacian(ref, c, v, start, count):
        center = ref[c, v, start : start + count]
        return (
            ref[c, v, start + 1 : start + 1 + count]
            + ref[c, v, start - 1 : start - 1 + count]
            + pltpu.roll(center, 1, 1)
            + pltpu.roll(center, 127, 1)
            - 4.0 * center
        )

    for c in range(3):
        for v in range(2):
            first_ref[c, v, 8 : 8 + rows] = laplacian(padded_ref, c, v, 8, rows)
            first_ref[c, v, 7:8] = laplacian(padded_ref, c, v, 7, 1) * inside[0]
            first_ref[c, v, 8 + rows : 9 + rows] = (
                laplacian(padded_ref, c, v, 8 + rows, 1) * inside[1]
            )
            force_ref[c, v] = tension_ref[v] * first_ref[
                c, v, 8 : 8 + rows
            ] - bending_ref[v] * laplacian(first_ref, c, v, 8, rows)

    parts = []
    for ref in (force_ref, offset_ref):
        for c in range(3):
            value = ref[c].reshape(2 * rows, 128)
            high = value.astype(BF16).astype(F32)
            parts += [high, value - high]
    cell = cell_ref[...]
    parts += [
        ((cell >> 8) & 255).astype(F32),
        (cell & 255).astype(F32),
        (cell >> 16).astype(F32) + 1.0,
    ]
    slots = iota((SLOTS, 128), 0)
    owners = iota((DEVICES, 128), 0)
    for row in range(2 * rows):
        lanes = pl.ds(row * 128, 128)
        here = slots == slot_ref[row : row + 1]
        for n, part in enumerate(parts):
            left_ref[n * SLOTS : (n + 1) * SLOTS, lanes] = jnp.where(
                here, part[row : row + 1], 0.0
            ).astype(BF16)
        right_ref[:, lanes] = jnp.where(owners == owner_ref[row : row + 1], 1.0, 0.0).astype(BF16)
    placed = lax.dot_general(left_ref[...], right_ref[...], NT, preferred_element_type=F32)
    group = [placed[n * SLOTS : (n + 1) * SLOTS] for n in range(len(parts))]
    values = [group[2 * n] + group[2 * n + 1] for n in range(6)]
    code = jnp.where(
        group[14] > 0.5, (group[14] - 1.0) * 65536.0 + group[12] * 256.0 + group[13] + 1.0, 0.0
    )
    send_ref[:, 0, :] = jnp.concatenate(values + [code], 0).T


GROUP = 8


def spread_source(points_ref, source, targets, listed_ref, total, buffers, add):
    rows16 = iota((16, 128), 0)

    def windows(base, weights):
        low = base & 15
        pieces = []
        for shift in (0, 16):
            near = rows16 + shift - low
            piece = jnp.zeros((16, 128), F32)
            for tap in range(4):
                piece = jnp.where(near == tap, weights[tap], piece)
            pieces.append(piece)
        return pieces

    def build(index, left_ref, right_ref):
        step = listed_ref[jnp.minimum(index, total)]
        used = (index < total).astype(F32)

        def item(n):
            return points_ref[pl.ds(pl.multiple_of(n * SLOTS + step * GROUP, GROUP), GROUP), :]

        cell = item(6).astype(jnp.int32) - 1
        plane = cell >> 16
        base_x = (((cell >> 8) & 255) - 1) & 255
        base_y = ((cell & 255) - 1) & 255
        taps = []
        for c in range(3):
            angle = item(3 + c) * (0.5 * math.pi)
            cosine, sine = 0.25 * jnp.cos(angle), 0.25 * jnp.sin(angle)
            taps.append([0.25 - sine, 0.25 + cosine, 0.25 + sine, 0.25 - cosine])
        scaled = []
        for target in targets:

            def weight(from_plane):
                reach = target - from_plane - 2 * source
                return taps[2][reach + 1] if -1 <= reach <= 2 else jnp.zeros((GROUP, 128), F32)

            weight_z = jnp.where(plane == 0, weight(0), weight(1)) * used
            scaled += [item(c) * weight_z for c in range(3)]
        high_x = (base_x >> 4).astype(F32)
        high_y = (base_y >> 4).astype(F32)
        zero = jnp.zeros((16, 128), BF16)

        def slice_of(r):
            lanes = pl.ds(r * 128, 128)

            def at(value):
                return jnp.broadcast_to(value[r : r + 1], (16, 128))

            near_x = windows(at(base_x), [at(t) for t in taps[0]])
            near_y = [p.astype(BF16) for p in windows(at(base_y), [at(t) for t in taps[1]])]
            left = [[(at(s) * piece).astype(BF16) for piece in near_x] for s in scaled]
            block_x = at(high_x).astype(BF16)
            block_y = at(high_y).astype(BF16)
            is_x = [block_x == jnp.asarray(g, BF16) for g in range(16)]
            is_y = [block_y == jnp.asarray(g, BF16) for g in range(16)]
            for g in range(16):
                right_ref[16 * g : 16 * g + 16, lanes] = jnp.where(
                    is_y[g], near_y[0], jnp.where(is_y[g - 1], near_y[1], zero)
                )
                for n, (low, high) in enumerate(left):
                    left_ref[pl.ds(256 * n + 16 * g, 16), lanes] = jnp.where(
                        is_x[g], low, jnp.where(is_x[g - 1], high, zero)
                    )

        return slice_of

    rows = 768 * len(targets)
    first = targets[0] * 768

    def product(left_ref, right_ref, n):
        add(
            first + 256 * n,
            256,
            lax.dot_general(
                left_ref[256 * n : 256 * n + 256], right_ref[...], NT, preferred_element_type=F32
            ),
        )

    (left_0, right_0), (left_1, right_1) = buffers
    parts = 3 * len(targets)

    def both(left_a, right_a, index, left_b, right_b):
        slice_of = build(index, left_b, right_b)
        done = 0
        for n in range(parts):
            product(left_a, right_a, n)
            while done * parts < (n + 1) * GROUP and done < GROUP:
                slice_of(done)
                done += 1

    @pl.when(total > 0)
    def _():
        slice_of = build(0, left_0, right_0)
        for r in range(GROUP):
            slice_of(r)

        @pl.loop(0, (total + 1) >> 1)
        def _(turn):
            both(left_0, right_0, 2 * turn + 1, left_1, right_1)
            both(left_1, right_1, 2 * turn + 2, left_0, right_0)


def listed(points_ref, listed_ref, wanted):
    total = jnp.int32(0)
    for step in range(SLOTS // GROUP):
        start = 6 * SLOTS + step * GROUP
        found = wanted(points_ref[start : start + GROUP, :])
        listed_ref[total] = step
        total = total + found.astype(jnp.int32)
    listed_ref[total] = 0
    return total


def has_plane_0(code):
    return jnp.max(jnp.where((code > 0.5) & (code < 65536.5), 1.0, 0.0)) > 0.5


def has_plane_1(code):
    return jnp.max(code) > 65536.5


def only_plane_0(code):
    most = jnp.max(code)
    return (most > 0.5) & (most < 65536.5)


def spread_own_kernel(own_ref, field_ref, points_ref, left_0, right_0, left_1, right_1, list_ref):
    points_ref[...] = own_ref[...].T
    field_ref[...] = jnp.zeros_like(field_ref)

    def add(first, rows, value):
        field_ref[first : first + rows] += value

    buffers = ((left_0, right_0), (left_1, right_1))
    total = listed(points_ref, list_ref, lambda code: jnp.max(code) > 0.5)
    spread_source(points_ref, 0, (0, 1), list_ref, total, buffers, add)


def spread_own(own):
    return pl.pallas_call(
        spread_own_kernel,
        out_shape=jax.ShapeDtypeStruct((1536, WIDTH), F32),
        in_specs=[VMEM],
        out_specs=VMEM,
        scratch_shapes=spread_scratch(),
        compiler_params=params(14),
        cost_estimate=cost(10),
        name="spread_own",
    )(own)


def spread_scratch():
    return [pltpu.VMEM((7 * SLOTS, 128), F32)] + [
        pltpu.VMEM((1536, 128 * GROUP), BF16),
        pltpu.VMEM((256, 128 * GROUP), BF16),
    ] * 2 + [pltpu.SMEM((SLOTS // GROUP + 1,), jnp.int32)]


def signed(item, vector):
    total = None
    for sign, value in zip((velocity_x[item], velocity_y[item], velocity_z[item]), vector):
        if sign:
            value = value if sign > 0 else -value
            total = value if total is None else total + value
    return total


def post_collision(current, push):
    density = current[0]
    for item in range(1, 19):
        density = density + current[item]
    moment = []
    for table in (velocity_x, velocity_y, velocity_z):
        plus = [current[i] for i in range(19) if table[i] > 0]
        minus = [current[i] for i in range(19) if table[i] < 0]
        moment.append(functools.reduce(jnp.add, plus) - functools.reduce(jnp.add, minus))
    inverse = 1.0 / density
    rate = 1.0 / relax_time
    half = 1.0 - 0.5 * rate
    flux = [m + 0.5 * f for m, f in zip(moment, push)]
    flow = [j * inverse for j in flux]
    rest = rate * density
    for u, j, f in zip(flow, flux, push):
        rest = rest - u * ((1.5 * rate) * j + (3.0 * half) * f)
    linear = [(3.0 * rate) * j + (3.0 * half) * f for j, f in zip(flux, push)]
    square = [(4.5 * rate) * j + (9.0 * half) * f for j, f in zip(flux, push)]
    result = [None] * 19
    result[10] = (1.0 - rate) * current[10] + (1.0 / 3) * rest
    for one, other in pairs:
        weight = 1.0 / 18 if one in (0, 11, 13) else 1.0 / 36
        even = weight * (rest + signed(one, flow) * signed(one, square))
        odd = weight * signed(one, linear)
        result[one] = (1.0 - rate) * current[one] + (even + odd)
        result[other] = (1.0 - rate) * current[other] + (even - odd)
    return result


def row_loads(start, rows, moves, sem):
    spans = [(start - 8, rows + 16, 0)]
    if start == 0:
        spans = [(WIDTH - 8, 8, 0), (0, rows + 8, 8)]
    elif start + rows == WIDTH:
        spans = [(start - 8, rows + 8, 0), (0, 8, rows + 8)]
    loads = []
    for z in range(2):
        group = []
        for n, (source, target) in enumerate(moves):
            for k, (first, count, place) in enumerate(spans):
                group.append(
                    pltpu.make_async_copy(
                        source.at[z, :, pl.ds(first, count)],
                        target.at[z, :, pl.ds(place, count)],
                        sem.at[z, n, k],
                    )
                )
        loads.append(group)
    for copy in loads[0] + loads[1]:
        copy.start()
    return loads


def collide_rows(
    start, rows, loads, current_ref, push_of, moved_ref, up_ref, down_ref, out_ref, carry_ref, out_sem
):
    stores = []
    row = iota((8, WIDTH), 0)
    for z in range(2):
        for copy in loads[z]:
            copy.wait()

        @pl.loop(0, rows // 8 + 2, unroll=3)
        def _(step):
            here = pl.multiple_of(step * 8, 8)
            now = pl.multiple_of(step * 8 + 8, 8)
            current = [current_ref[z, i, pl.ds(here, 8), :] for i in range(19)]
            result = post_collision(current, push_of(z, step))
            slot = 0
            for i in range(19):
                value = result[i]
                if velocity_y[i]:
                    value = pltpu.roll(value, velocity_y[i] % WIDTH, 1)
                if velocity_x[i] == 0:
                    out_ref[z, i, pl.ds(now, 8), :] = value
                    continue
                value = pltpu.roll(value, velocity_x[i] % 8, 0)
                old = carry_ref[slot]
                carry_ref[slot] = value
                slot += 1
                if velocity_x[i] > 0:
                    out_ref[z, i, pl.ds(now, 8), :] = jnp.where(row == 0, old, value)
                else:
                    out_ref[z, i, pl.ds(here, 8), :] = jnp.where(row == 7, value, old)

        within = pl.ds(start, rows)
        for n, (low, high, place) in enumerate(
            (
                (0, 5, moved_ref.at[1, 0:5, within] if z == 0 else up_ref),
                (5, 10, moved_ref.at[0, 5:10, within] if z == 1 else down_ref),
                (10, 19, moved_ref.at[z, 10:19, within]),
            )
        ):
            copy = pltpu.make_async_copy(
                out_ref.at[z, low:high, pl.ds(16, rows)], place, out_sem.at[z, n]
            )
            copy.start()
            stores.append(copy)
    for copy in stores:
        copy.wait()


def collide_scratch(rows):
    return [
        pltpu.VMEM((2, 19, rows + 16, WIDTH), F32),
        pltpu.VMEM((2, 19, rows + 24, WIDTH), F32),
        pltpu.VMEM((10, 8, WIDTH), F32),
        pltpu.SemaphoreType.DMA((2, 2, 2)),
        pltpu.SemaphoreType.DMA((2, 3)),
    ]


def collide_shapes(rows):
    return (
        jax.ShapeDtypeStruct((2, 19, WIDTH, WIDTH), F32),
        jax.ShapeDtypeStruct((5, rows, WIDTH), F32),
        jax.ShapeDtypeStruct((5, rows, WIDTH), F32),
    )


def collide_kernel(
    start,
    rows,
    populations_ref,
    field_ref,
    held_ref,
    moved_ref,
    up_ref,
    down_ref,
    push_ref,
    current_ref,
    out_ref,
    carry_ref,
    in_sem,
    out_sem,
):
    loads = row_loads(
        start, rows, ((populations_ref, current_ref), (field_ref, push_ref)), in_sem
    )

    def push_of(z, step):
        return [push_ref[z, c, pl.ds(pl.multiple_of(step * 8, 8), 8), :] for c in range(3)]

    collide_rows(
        start,
        rows,
        loads,
        current_ref,
        push_of,
        moved_ref,
        up_ref,
        down_ref,
        out_ref,
        carry_ref,
        out_sem,
    )


def collide(start, rows, populations, field, held):
    return pl.pallas_call(
        functools.partial(collide_kernel, start, rows),
        out_shape=collide_shapes(rows),
        in_specs=[HBM, HBM, ANY],
        out_specs=(ANY, VMEM, VMEM),
        scratch_shapes=[pltpu.VMEM((2, 3, rows + 16, WIDTH), F32)] + collide_scratch(rows),
        input_output_aliases={2: 0},
        compiler_params=params(50),
        cost_estimate=cost(9),
        name="collide",
    )(populations, field, held)


def spread_near_kernel(
    rows,
    below_ref,
    above_ref,
    held_ref,
    populations_ref,
    field_to,
    moved_ref,
    up_ref,
    down_ref,
    field_ref,
    points_ref,
    left_0,
    right_0,
    left_1,
    right_1,
    list_ref,
    field_sem,
    current_ref,
    out_ref,
    carry_ref,
    in_sem,
    out_sem,
):
    loads = row_loads(0, rows, ((populations_ref, current_ref),), in_sem)

    def add(first, count, value):
        field_ref[first : first + count] += value

    buffers = ((left_0, right_0), (left_1, right_1))
    field_ref[...] = held_ref[...]
    points_ref[...] = below_ref[...].T
    total = listed(points_ref, list_ref, has_plane_1)
    spread_source(points_ref, -1, (0, 1), list_ref, total, buffers, add)
    total = listed(points_ref, list_ref, only_plane_0)
    spread_source(points_ref, -1, (0,), list_ref, total, buffers, add)
    points_ref[...] = above_ref[...].T
    total = listed(points_ref, list_ref, has_plane_0)
    spread_source(points_ref, 1, (1,), list_ref, total, buffers, add)
    store = pltpu.make_async_copy(field_ref, field_to, field_sem)
    store.start()

    def push_of(z, step):
        place = (step * 8 + WIDTH - 8) & (WIDTH - 1)
        return [
            field_ref[pl.ds(pl.multiple_of((3 * z + c) * WIDTH + place, 8), 8), :]
            for c in range(3)
        ]

    collide_rows(
        0,
        rows,
        loads,
        current_ref,
        push_of,
        moved_ref,
        up_ref,
        down_ref,
        out_ref,
        carry_ref,
        out_sem,
    )
    store.wait()


def spread_near(rows, below, above, field, populations):
    return pl.pallas_call(
        functools.partial(spread_near_kernel, rows),
        out_shape=(jax.ShapeDtypeStruct((1536, WIDTH), F32),) + collide_shapes(rows),
        in_specs=[VMEM] * 3 + [HBM],
        out_specs=(HBM, ANY, VMEM, VMEM),
        scratch_shapes=[pltpu.VMEM((1536, WIDTH), F32)]
        + spread_scratch()
        + [pltpu.SemaphoreType.DMA]
        + collide_scratch(rows),
        compiler_params=params(50),
        cost_estimate=cost(18),
        name="spread_near",
    )(below, above, field, populations)


def place_kernel(starts, *refs):
    count = len(starts)
    ups, downs = refs[:count], refs[count : 2 * count]
    moved_ref, sem = refs[2 * count + 1 :]
    copies = []
    for n, start in enumerate(starts):
        within = pl.ds(start, ups[n].shape[1])
        copies += [
            pltpu.make_async_copy(ups[n], moved_ref.at[0, 0:5, within], sem.at[0, n]),
            pltpu.make_async_copy(downs[n], moved_ref.at[1, 5:10, within], sem.at[1, n]),
        ]
    for copy in copies:
        copy.start()
    for copy in copies:
        copy.wait()


def place(starts, ups, downs, moved):
    count = len(starts)
    return pl.pallas_call(
        functools.partial(place_kernel, starts),
        out_shape=jax.ShapeDtypeStruct(moved.shape, F32),
        in_specs=[VMEM] * (2 * count) + [ANY],
        out_specs=ANY,
        scratch_shapes=[pltpu.SemaphoreType.DMA((2, count))],
        input_output_aliases={2 * count: 0},
        compiler_params=params(8),
        cost_estimate=cost(1),
        name="place",
    )(*ups, *downs, moved)


def passed_along(value, steps, axis=("ves", "shard"), wrap=True):
    count = math.prod(lax.axis_size(a) for a in axis)
    return lax.ppermute(
        value,
        axis,
        [(i, (i + steps) % count) for i in range(count) if wrap or 0 <= i + steps < count],
    )


def cost(microseconds):
    return pl.CostEstimate(
        flops=microseconds * 10**9, bytes_accessed=microseconds * 10**6, transcendentals=0
    )


def params(megabytes):
    return pltpu.CompilerParams(vmem_limit_bytes=megabytes * 1024 * 1024)


def on_device(displacement, tension, bending, offset, owner, cell, populations):
    shape = jax.ShapeDtypeStruct
    before = passed_along(displacement[:, :, -2:], 1, ("shard",), False)
    after = passed_along(displacement[:, :, :2], -1, ("shard",), False)
    owner_rows = owner.reshape(32, 128)
    cell_rows = cell.reshape(32, 128)
    slot = pl.pallas_call(
        rank_kernel,
        out_shape=shape((32, 128), jnp.int32),
        in_specs=[HBM] * 2,
        out_specs=VMEM,
        scratch_shapes=[
            pltpu.VMEM((32, 128), jnp.int32),
            pltpu.VMEM((32, 128), jnp.int32),
            pltpu.SemaphoreType.DMA((2,)),
        ],
        compiler_params=params(60),
        cost_estimate=cost(3),
        name="rank",
    )(owner_rows, cell_rows)
    membrane_force, send = pl.pallas_call(
        pack_kernel,
        out_shape=(shape((3, 2, 16, 128), F32), shape((DEVICES, 1, 7 * SLOTS), F32)),
        in_specs=[HBM] * 3 + [VMEM] * 2 + [HBM] * 3 + [VMEM],
        out_specs=(VMEM, VMEM),
        scratch_shapes=[
            pltpu.SMEM((2,), F32),
            pltpu.SMEM((2,), F32),
            pltpu.VMEM((3, 2, 16, 128), F32),
            pltpu.VMEM((32, 128), jnp.int32),
            pltpu.VMEM((32, 128), jnp.int32),
            pltpu.VMEM((3, 2, 32, 128), F32),
            pltpu.VMEM((3, 2, 32, 128), F32),
            pltpu.VMEM((15 * SLOTS, 4096), BF16),
            pltpu.VMEM((DEVICES, 4096), BF16),
            pltpu.SemaphoreType.DMA((6,)),
        ],
        compiler_params=params(60),
        cost_estimate=cost(5),
        name="pack",
    )(
        tension, bending, displacement, before, after, offset, owner_rows, cell_rows, slot
    )
    own = lax.all_to_all(send, ("ves", "shard"), split_axis=0, concat_axis=0, tiled=True)
    own = own.reshape(DEVICES, 7 * SLOTS)
    below = passed_along(own, 1)
    above = passed_along(own, -1)
    start = CHUNKS[0]
    field, moved, up, down = spread_near(start, below, above, spread_own(own), populations)
    force_field = field.reshape(2, 3, WIDTH, WIDTH)
    ups, downs, starts = [passed_along(up, 1)], [passed_along(down, -1)], [0]
    for rows in CHUNKS[1:]:
        moved, up, down = collide(start, rows, populations, force_field, moved)
        ups.append(passed_along(up, 1))
        downs.append(passed_along(down, -1))
        starts.append(start)
        start += rows
    moved = place(starts[:-1], ups[:-1], downs[:-1], moved)
    moved = place(starts[-1:], ups[-1:], downs[-1:], moved)
    return (membrane_force, force_field, moved)


def solution(mesh):
    return jax.shard_map(
        on_device,
        mesh=mesh,
        in_specs=(
            P(None, "ves", "shard", None),
            P("ves"),
            P("ves"),
            P(None, "ves", "shard", None),
            P("ves", "shard", None),
            P("ves", "shard", None),
            P(("ves", "shard"), None, None, None),
        ),
        out_specs=(
            P(None, "ves", "shard", None),
            P(("ves", "shard"), None, None, None),
            P(("ves", "shard"), None, None, None),
        ),
        check_vma=False,
    )
```

```python
import functools
import math

import jax
import jax.numpy as jnp
from jax import lax
from jax.experimental import pallas as pl
from jax.experimental.pallas import tpu as pltpu
from jax.sharding import PartitionSpec as P

relax_time = 0.8
velocity_x = [0, 1, -1, 0, 0, 0, 1, -1, 0, 0, 0, 1, -1, 0, 0, 1, 1, -1, -1]
velocity_y = [0, 0, 0, 1, -1, 0, 0, 0, 1, -1, 0, 0, 0, 1, -1, 1, -1, 1, -1]
velocity_z = [1, 1, 1, 1, 1, -1, -1, -1, -1, -1, 0, 0, 0, 0, 0, 0, 0, 0, 0]
pairs = [(0, 5), (1, 7), (2, 6), (3, 9), (4, 8), (11, 12), (13, 14), (15, 18), (16, 17)]
SLOTS = 64
DEVICES = 128
WIDTH = 256
F32 = jnp.float32
BF16 = jnp.bfloat16
VMEM = pl.BlockSpec(memory_space=pltpu.VMEM)
SMEM = pl.BlockSpec(memory_space=pltpu.SMEM)
ANY = pl.BlockSpec(memory_space=pl.ANY)
HBM = pl.BlockSpec(memory_space=pltpu.HBM)
HALF = 128
FIRST = (15, 0, 1, 2, 3, 4, 5, 6, 7, 8)
SECOND = (9, 10, 11, 12, 13, 14)
EVERY = tuple(range(16))
NT = (((1,), (1,)), ((), ()))


def iota(shape, dim):
    return lax.broadcasted_iota(jnp.int32, shape, dim)


def fetch(moves, sem):
    copies = [pltpu.make_async_copy(*move, sem.at[n]) for n, move in enumerate(moves)]
    for copy in copies:
        copy.start()
    for copy in copies:
        copy.wait()


def rank_kernel(owner_from, cell_from, slot_ref, owner_ref, cell_ref, sem):
    fetch(((owner_from, owner_ref), (cell_from, cell_ref)), sem)
    classes = 2 * DEVICES
    before = jnp.where(iota((256, 512), 0) < iota((256, 512), 1), 1.0, 0.0)
    before = before.astype(BF16)
    label = owner_ref[...] + DEVICES * (cell_ref[...] >> 16)
    carry = jnp.zeros((classes, 256), F32)
    rows = iota((classes, 128), 0)
    for k in range(label.shape[0] // 2):
        member = jnp.concatenate(
            [jnp.where(rows == label[2 * k + s : 2 * k + s + 1], 1.0, 0.0) for s in range(2)], 1
        )
        count = jnp.dot(member.astype(BF16), before, preferred_element_type=F32)
        place = jnp.sum(member * (count[:, :256] + carry), 0, keepdims=True)
        carry = carry + count[:, 256:]
        for s in range(2):
            slot_ref[2 * k + s : 2 * k + s + 1, :] = place[:, 128 * s : 128 * s + 128].astype(
                jnp.int32
            )
    place = slot_ref[...]
    slot_ref[...] = jnp.where(label < DEVICES, place, SLOTS - 1 - place)


def pack_kernel(
    tension_from,
    bending_from,
    displacement_from,
    before_ref,
    after_ref,
    offset_from,
    owner_from,
    cell_from,
    slot_ref,
    force_ref,
    send_ref,
    tension_ref,
    bending_ref,
    offset_ref,
    owner_ref,
    cell_ref,
    padded_ref,
    first_ref,
    left_ref,
    right_ref,
    sem,
):
    rows = displacement_from.shape[2]
    fetch(
        (
            (tension_from, tension_ref),
            (bending_from, bending_ref),
            (offset_from, offset_ref),
            (owner_from, owner_ref),
            (cell_from, cell_ref),
            (displacement_from, padded_ref.at[:, :, pl.ds(8, rows)]),
        ),
        sem,
    )
    here = lax.axis_index("shard")
    inside = ((here > 0).astype(F32), (here < lax.axis_size("shard") - 1).astype(F32))
    padded_ref[:, :, 6:8] = before_ref[...]
    padded_ref[:, :, 8 + rows : 10 + rows] = after_ref[...]

    def laplacian(ref, c, v, start, count):
        center = ref[c, v, start : start + count]
        return (
            ref[c, v, start + 1 : start + 1 + count]
            + ref[c, v, start - 1 : start - 1 + count]
            + pltpu.roll(center, 1, 1)
            + pltpu.roll(center, 127, 1)
            - 4.0 * center
        )

    for c in range(3):
        for v in range(2):
            first_ref[c, v, 8 : 8 + rows] = laplacian(padded_ref, c, v, 8, rows)
            first_ref[c, v, 7:8] = laplacian(padded_ref, c, v, 7, 1) * inside[0]
            first_ref[c, v, 8 + rows : 9 + rows] = (
                laplacian(padded_ref, c, v, 8 + rows, 1) * inside[1]
            )
            force_ref[c, v] = tension_ref[v] * first_ref[
                c, v, 8 : 8 + rows
            ] - bending_ref[v] * laplacian(first_ref, c, v, 8, rows)

    parts = []
    for ref in (force_ref, offset_ref):
        for c in range(3):
            value = ref[c].reshape(2 * rows, 128)
            high = value.astype(BF16).astype(F32)
            parts += [high, value - high]
    cell = cell_ref[...]
    parts += [
        ((cell >> 8) & 255).astype(F32),
        (cell & 255).astype(F32),
        (cell >> 16).astype(F32) + 1.0,
    ]
    slots = iota((SLOTS, 128), 0)
    owners = iota((DEVICES, 128), 0)
    for row in range(2 * rows):
        lanes = pl.ds(row * 128, 128)
        here = slots == slot_ref[row : row + 1]
        for n, part in enumerate(parts):
            left_ref[n * SLOTS : (n + 1) * SLOTS, lanes] = jnp.where(
                here, part[row : row + 1], 0.0
            ).astype(BF16)
        right_ref[:, lanes] = jnp.where(owners == owner_ref[row : row + 1], 1.0, 0.0).astype(BF16)
    placed = lax.dot_general(left_ref[...], right_ref[...], NT, preferred_element_type=F32)
    group = [placed[n * SLOTS : (n + 1) * SLOTS] for n in range(len(parts))]
    values = [group[2 * n] + group[2 * n + 1] for n in range(6)]
    code = jnp.where(
        group[14] > 0.5, (group[14] - 1.0) * 65536.0 + group[12] * 256.0 + group[13] + 1.0, 0.0
    )
    send_ref[:, 0, :] = jnp.concatenate(values + [code], 0).T


GROUP = 8


def spread_source(points_ref, targets, blocks, entry, total, buffers, add, tall=256):
    rows16 = iota((16, 128), 0)
    rows = 16 * len(blocks)

    def windows(base, weights):
        low = base & 15
        pieces = []
        for shift in (0, 16):
            near = rows16 + shift - low
            piece = jnp.zeros((16, 128), F32)
            for tap in range(4):
                piece = jnp.where(near == tap, weights[tap], piece)
            pieces.append(piece)
        return pieces

    def build(index, left_ref, right_ref):
        begin, weigh, _ = entry(jnp.minimum(index, total - 1))
        used = (index < total).astype(F32)

        def item(n):
            return points_ref[pl.ds(pl.multiple_of(n * SLOTS + begin, GROUP), GROUP), :]

        cell = item(6).astype(jnp.int32) - 1
        plane = cell >> 16
        base_x = (((cell >> 8) & 255) - 1) & 255
        base_y = ((cell & 255) - 1) & 255
        taps = []
        for c in range(3):
            angle = item(3 + c) * (0.5 * math.pi)
            cosine, sine = 0.25 * jnp.cos(angle), 0.25 * jnp.sin(angle)
            taps.append([0.25 - sine, 0.25 + cosine, 0.25 + sine, 0.25 - cosine])
        scaled = []
        for weight_z in weigh(plane, taps[2]):
            weight_z = weight_z * used
            scaled += [item(c) * weight_z for c in range(3)]
        high_x = (base_x >> 4).astype(F32)
        high_y = (base_y >> 4).astype(F32)
        zero = jnp.zeros((16, 128), BF16)

        def slice_of(r):
            lanes = pl.ds(r * 128, 128)

            def at(value):
                return jnp.broadcast_to(value[r : r + 1], (16, 128))

            near_x = windows(at(base_x), [at(t) for t in taps[0]])
            near_y = [p.astype(BF16) for p in windows(at(base_y), [at(t) for t in taps[1]])]
            left = [[(at(s) * piece).astype(BF16) for piece in near_x] for s in scaled]
            block_x = at(high_x).astype(BF16)
            block_y = at(high_y).astype(BF16)
            is_x = [block_x == jnp.asarray(g, BF16) for g in range(16)]
            is_y = [block_y == jnp.asarray(g, BF16) for g in range(16)]
            for g in range(16):
                right_ref[16 * g : 16 * g + 16, lanes] = jnp.where(
                    is_y[g], near_y[0], jnp.where(is_y[g - 1], near_y[1], zero)
                )
            for k, g in enumerate(blocks):
                for n, (low, high) in enumerate(left):
                    left_ref[pl.ds(rows * n + 16 * k, 16), lanes] = jnp.where(
                        is_x[g], low, jnp.where(is_x[g - 1], high, zero)
                    )

        return slice_of

    height = 3 * rows * targets
    parts = max(1, (height + tall // 2) // tall)

    def product(index, left_ref, right_ref, n):
        first = 0 if targets == 2 else 3 * rows * entry(jnp.minimum(index, total - 1))[2]
        low = tall * n
        high = height if n == parts - 1 else low + tall
        add(
            low if targets == 2 else pl.multiple_of(first + low, 8),
            high - low,
            lax.dot_general(
                left_ref[low:high], right_ref[...], NT, preferred_element_type=F32
            ),
        )

    (left_0, right_0), (left_1, right_1) = buffers

    def both(left_a, right_a, index, left_b, right_b):
        slice_of = build(index, left_b, right_b)
        done = 0
        for n in range(parts):
            product(index - 1, left_a, right_a, n)
            while done * parts < (n + 1) * GROUP and done < GROUP:
                slice_of(done)
                done += 1

    @pl.when(total > 0)
    def _():
        slice_of = build(0, left_0, right_0)
        for r in range(GROUP):
            slice_of(r)

        @pl.loop(0, (total + 1) >> 1)
        def _(turn):
            both(left_0, right_0, 2 * turn + 1, left_1, right_1)
            both(left_1, right_1, 2 * turn + 2, left_0, right_0)


def filled(points_ref, begin):
    code = points_ref[begin + 6 * SLOTS : begin + 7 * SLOTS, :]
    slot = iota(code.shape, 0).astype(F32)
    most = jnp.max(jnp.where((code > 0.5) & (code < 65536.5), slot + 1.0, 0.0))
    least = jnp.min(jnp.where(code > 65536.5, slot, float(SLOTS)))
    low = (most.astype(jnp.int32) + GROUP - 1) // GROUP
    return low, least.astype(jnp.int32) // GROUP


def weights_at(source, targets):
    def weigh(plane, taps):
        found = []
        for target in targets:
            pair = []
            for from_plane in range(2):
                reach = target - from_plane - 2 * source
                pair.append(taps[reach + 1] if -1 <= reach <= 2 else jnp.zeros_like(taps[0]))
            found.append(jnp.where(plane == 0, *pair))
        return found

    return weigh


def spread_own_points(own_ref, blocks, points_ref, buffers, add):
    points_ref[0 : 7 * SLOTS] = own_ref[...].T
    low, high = filled(points_ref, 0)
    high = jnp.maximum(low, high)

    def entry(index):
        step = jnp.where(index < low, index, high + index - low)
        return step * GROUP, weights_at(0, (0, 1)), 0

    total = low + SLOTS // GROUP - high
    spread_source(points_ref, 2, blocks, entry, total, buffers, add, 768)


def spread_near_points(below_ref, above_ref, blocks, points_ref, buffers, add):
    points_ref[0 : 7 * SLOTS] = below_ref[...].T
    points_ref[7 * SLOTS : 14 * SLOTS] = above_ref[...].T
    low, high = filled(points_ref, 0)
    low_above, _ = filled(points_ref, 7 * SLOTS)

    def entry(index):
        return (high + index) * GROUP, weights_at(-1, (0, 1)), 0

    spread_source(points_ref, 2, blocks, entry, SLOTS // GROUP - high, buffers, add)
    count = jnp.minimum(low, high)

    def entry_of_one(index):
        above = index >= count
        step = jnp.where(above, index - count, index)

        def weigh(plane, taps):
            return [jnp.where(plane == 0, jnp.where(above, taps[0], taps[3]), 0.0)]

        return (
            jnp.where(above, 7 * SLOTS, 0) + step * GROUP,
            weigh,
            jnp.where(above, 1, 0),
        )

    spread_source(points_ref, 1, blocks, entry_of_one, count + low_above, buffers, add)


def spread_scratch(blocks):
    return [pltpu.VMEM((14 * SLOTS, 128), F32)] + [
        pltpu.VMEM((96 * len(blocks), 128 * GROUP), BF16),
        pltpu.VMEM((256, 128 * GROUP), BF16),
    ] * 2


def spread_own_kernel(own_ref, field_ref, points_ref, left_0, right_0, left_1, right_1):
    field_ref[...] = jnp.zeros_like(field_ref)

    def add(first, count, value):
        field_ref[pl.ds(first, count)] += value

    buffers = ((left_0, right_0), (left_1, right_1))
    spread_own_points(own_ref, EVERY, points_ref, buffers, add)


def spread_own(own):
    return pl.pallas_call(
        spread_own_kernel,
        out_shape=jax.ShapeDtypeStruct((6 * WIDTH, WIDTH), F32),
        in_specs=[VMEM],
        out_specs=VMEM,
        scratch_shapes=spread_scratch(EVERY),
        compiler_params=params(14),
        cost_estimate=cost(8),
        name="spread_own",
    )(own)


def signed(item, vector):
    total = None
    for sign, value in zip((velocity_x[item], velocity_y[item], velocity_z[item]), vector):
        if sign:
            value = value if sign > 0 else -value
            total = value if total is None else total + value
    return total


def post_collision(current, push):
    density = current[0]
    for item in range(1, 19):
        density = density + current[item]
    moment = []
    for table in (velocity_x, velocity_y, velocity_z):
        plus = [current[i] for i in range(19) if table[i] > 0]
        minus = [current[i] for i in range(19) if table[i] < 0]
        moment.append(functools.reduce(jnp.add, plus) - functools.reduce(jnp.add, minus))
    inverse = 1.0 / density
    rate = 1.0 / relax_time
    half = 1.0 - 0.5 * rate
    flux = [m + 0.5 * f for m, f in zip(moment, push)]
    flow = [j * inverse for j in flux]
    rest = rate * density
    for u, j, f in zip(flow, flux, push):
        rest = rest - u * ((1.5 * rate) * j + (3.0 * half) * f)
    linear = [(3.0 * rate) * j + (3.0 * half) * f for j, f in zip(flux, push)]
    square = [(4.5 * rate) * j + (9.0 * half) * f for j, f in zip(flux, push)]
    result = [None] * 19
    result[10] = (1.0 - rate) * current[10] + (1.0 / 3) * rest
    for one, other in pairs:
        weight = 1.0 / 18 if one in (0, 11, 13) else 1.0 / 36
        even = weight * (rest + signed(one, flow) * signed(one, square))
        odd = weight * signed(one, linear)
        result[one] = (1.0 - rate) * current[one] + (even + odd)
        result[other] = (1.0 - rate) * current[other] + (even - odd)
    return result


def row_loads(start, rows, source, target, sem):
    spans = [(start - 8, rows + 16, 0)]
    if start == 0:
        spans = [(WIDTH - 8, 8, 0), (0, rows + 8, 8)]
    elif start + rows == WIDTH:
        spans = [(start - 8, rows + 8, 0), (0, 8, rows + 8)]
    loads = [
        [
            pltpu.make_async_copy(
                source.at[z, :, pl.ds(first, count)],
                target.at[z, :, pl.ds(place, count)],
                sem.at[z, k],
            )
            for k, (first, count, place) in enumerate(spans)
        ]
        for z in range(2)
    ]
    for copy in loads[0] + loads[1]:
        copy.start()
    return loads


def collide_rows(
    start, rows, loads, current_ref, push_of, moved_ref, up_ref, down_ref, out_ref, carry_ref, out_sem
):
    stores = []
    row = iota((8, WIDTH), 0)
    for z in range(2):
        for copy in loads[z]:
            copy.wait()

        @pl.loop(0, rows // 8 + 2, unroll=3)
        def _(step):
            here = pl.multiple_of(step * 8, 8)
            now = pl.multiple_of(step * 8 + 8, 8)
            current = [current_ref[z, i, pl.ds(here, 8), :] for i in range(19)]
            result = post_collision(current, push_of(z, step))
            slot = 0
            for i in range(19):
                value = result[i]
                if velocity_y[i]:
                    value = pltpu.roll(value, velocity_y[i] % WIDTH, 1)
                if velocity_x[i] == 0:
                    out_ref[z, i, pl.ds(now, 8), :] = value
                    continue
                value = pltpu.roll(value, velocity_x[i] % 8, 0)
                old = carry_ref[slot]
                carry_ref[slot] = value
                slot += 1
                if velocity_x[i] > 0:
                    out_ref[z, i, pl.ds(now, 8), :] = jnp.where(row == 0, old, value)
                else:
                    out_ref[z, i, pl.ds(here, 8), :] = jnp.where(row == 7, value, old)

        within = pl.ds(start, rows)
        for n, (low, high, place) in enumerate(
            (
                (0, 5, moved_ref.at[1, 0:5, within] if z == 0 else up_ref),
                (5, 10, moved_ref.at[0, 5:10, within] if z == 1 else down_ref),
                (10, 19, moved_ref.at[z, 10:19, within]),
            )
        ):
            copy = pltpu.make_async_copy(
                out_ref.at[z, low:high, pl.ds(16, rows)], place, out_sem.at[z, n]
            )
            copy.start()
            stores.append(copy)
    for copy in stores:
        copy.wait()


def collide_scratch(rows):
    return [
        pltpu.VMEM((2, 19, rows + 16, WIDTH), F32),
        pltpu.VMEM((2, 19, rows + 24, WIDTH), F32),
        pltpu.VMEM((10, 8, WIDTH), F32),
        pltpu.SemaphoreType.DMA((2, 2)),
        pltpu.SemaphoreType.DMA((2, 3)),
    ]


def collide_shapes(rows):
    return (
        jax.ShapeDtypeStruct((2, 19, WIDTH, WIDTH), F32),
        jax.ShapeDtypeStruct((5, rows, WIDTH), F32),
        jax.ShapeDtypeStruct((5, rows, WIDTH), F32),
    )


def first_half_kernel(
    below_ref,
    above_ref,
    held_ref,
    populations_ref,
    field_ref,
    field_to,
    moved_ref,
    up_ref,
    down_ref,
    points_ref,
    left_0,
    right_0,
    left_1,
    right_1,
    field_sem,
    current_ref,
    out_ref,
    carry_ref,
    in_sem,
    out_sem,
):
    loads = row_loads(0, HALF, populations_ref, current_ref, in_sem)
    size = 16 * len(FIRST)
    for n in range(6):
        field_ref[n * size : n * size + 16] = held_ref[n * WIDTH + WIDTH - 16 : n * WIDTH + WIDTH]
        field_ref[n * size + 16 : n * size + size] = held_ref[n * WIDTH : n * WIDTH + size - 16]

    def add(first, count, value):
        field_ref[pl.ds(first, count)] += value

    buffers = ((left_0, right_0), (left_1, right_1))
    spread_near_points(below_ref, above_ref, FIRST, points_ref, buffers, add)
    last, count = 16 * FIRST[0], 16 * len(FIRST) - 16
    stores = []
    for n in range(6):
        for k, (place, to, size) in enumerate(((0, last, 16), (16, 0, count))):
            stores.append(
                pltpu.make_async_copy(
                    field_ref.at[pl.ds(n * (count + 16) + place, size)],
                    field_to.at[n, pl.ds(to, size)],
                    field_sem.at[n, k],
                )
            )
    for copy in stores:
        copy.start()

    def push_of(z, step):
        rows = 16 * len(FIRST)
        return [
            field_ref[pl.ds(pl.multiple_of((3 * z + c) * rows + 8 + step * 8, 8), 8), :]
            for c in range(3)
        ]

    collide_rows(
        0, HALF, loads, current_ref, push_of, moved_ref, up_ref, down_ref, out_ref, carry_ref, out_sem
    )
    for copy in stores:
        copy.wait()


def first_half(below, above, field, populations):
    return pl.pallas_call(
        first_half_kernel,
        out_shape=(
            jax.ShapeDtypeStruct((96 * len(FIRST), WIDTH), F32),
            jax.ShapeDtypeStruct((6, WIDTH, WIDTH), F32),
        )
        + collide_shapes(HALF),
        in_specs=[VMEM] * 3 + [HBM],
        out_specs=(VMEM, ANY, ANY, VMEM, VMEM),
        scratch_shapes=spread_scratch(FIRST)
        + [pltpu.SemaphoreType.DMA((6, 2))]
        + collide_scratch(HALF),
        compiler_params=params(50),
        cost_estimate=cost(14),
        name="first_half",
    )(below, above, field, populations)


def second_half_kernel(
    below_ref,
    above_ref,
    held_ref,
    first_ref,
    populations_ref,
    field_held,
    moved_held,
    field_to,
    moved_ref,
    up_ref,
    down_ref,
    push_ref,
    field_ref,
    points_ref,
    left_0,
    right_0,
    left_1,
    right_1,
    field_sem,
    current_ref,
    out_ref,
    carry_ref,
    in_sem,
    out_sem,
):
    loads = row_loads(HALF, WIDTH - HALF, populations_ref, current_ref, in_sem)
    rows = 16 * len(SECOND)
    middle = 16 * SECOND[0] - HALF + 8
    after = middle + rows
    rest = push_ref.shape[1] - after
    for n in range(6):
        start = n * 16 * len(FIRST)
        push_ref[n, 0:middle] = first_ref[start + HALF + 8 : start + HALF + 8 + middle]
        push_ref[n, after:] = first_ref[start : start + rest]

    for n in range(6):
        start = n * WIDTH + 16 * SECOND[0]
        field_ref[n * rows : n * rows + rows] = held_ref[start : start + rows]

    def add(first, count, value):
        field_ref[pl.ds(first, count)] += value

    buffers = ((left_0, right_0), (left_1, right_1))
    spread_near_points(below_ref, above_ref, SECOND, points_ref, buffers, add)
    for n in range(6):
        push_ref[n, middle:after] = field_ref[n * rows : n * rows + rows]
    store = pltpu.make_async_copy(
        push_ref.at[:, pl.ds(middle, rows)],
        field_to.at[:, pl.ds(16 * SECOND[0], rows)],
        field_sem,
    )
    store.start()

    def push_of(z, step):
        place = pl.ds(pl.multiple_of(step * 8, 8), 8)
        return [push_ref[3 * z + c, place, :] for c in range(3)]

    collide_rows(
        HALF,
        WIDTH - HALF,
        loads,
        current_ref,
        push_of,
        moved_ref,
        up_ref,
        down_ref,
        out_ref,
        carry_ref,
        out_sem,
    )
    store.wait()


def second_half(below, above, held, first, populations, field, moved):
    rows = WIDTH - HALF
    return pl.pallas_call(
        second_half_kernel,
        out_shape=(jax.ShapeDtypeStruct((6, WIDTH, WIDTH), F32),) + collide_shapes(rows),
        in_specs=[VMEM] * 4 + [HBM, ANY, ANY],
        out_specs=(ANY, ANY, VMEM, VMEM),
        scratch_shapes=[
            pltpu.VMEM((6, rows + 16, WIDTH), F32),
            pltpu.VMEM((96 * len(SECOND), WIDTH), F32),
        ]
        + spread_scratch(SECOND)
        + [pltpu.SemaphoreType.DMA]
        + collide_scratch(rows),
        input_output_aliases={5: 0, 6: 1},
        compiler_params=params(50),
        cost_estimate=cost(18),
        name="second_half",
    )(below, above, held, first, populations, field, moved)


def place_kernel(starts, *refs):
    count = len(starts)
    ups, downs = refs[:count], refs[count : 2 * count]
    moved_ref, sem = refs[2 * count + 1 :]
    copies = []
    for n, start in enumerate(starts):
        within = pl.ds(start, ups[n].shape[1])
        copies += [
            pltpu.make_async_copy(ups[n], moved_ref.at[0, 0:5, within], sem.at[0, n]),
            pltpu.make_async_copy(downs[n], moved_ref.at[1, 5:10, within], sem.at[1, n]),
        ]
    for copy in copies:
        copy.start()
    for copy in copies:
        copy.wait()


def place(starts, ups, downs, moved):
    count = len(starts)
    return pl.pallas_call(
        functools.partial(place_kernel, starts),
        out_shape=jax.ShapeDtypeStruct(moved.shape, F32),
        in_specs=[VMEM] * (2 * count) + [ANY],
        out_specs=ANY,
        scratch_shapes=[pltpu.SemaphoreType.DMA((2, count))],
        input_output_aliases={2 * count: 0},
        compiler_params=params(8),
        cost_estimate=cost(1),
        name="place",
    )(*ups, *downs, moved)


def passed_along(value, steps, axis=("ves", "shard"), wrap=True):
    count = math.prod(lax.axis_size(a) for a in axis)
    return lax.ppermute(
        value,
        axis,
        [(i, (i + steps) % count) for i in range(count) if wrap or 0 <= i + steps < count],
    )


def cost(microseconds):
    return pl.CostEstimate(
        flops=microseconds * 10**9, bytes_accessed=microseconds * 10**6, transcendentals=0
    )


def params(megabytes):
    return pltpu.CompilerParams(vmem_limit_bytes=megabytes * 1024 * 1024)


def on_device(displacement, tension, bending, offset, owner, cell, populations):
    shape = jax.ShapeDtypeStruct
    before = passed_along(displacement[:, :, -2:], 1, ("shard",), False)
    after = passed_along(displacement[:, :, :2], -1, ("shard",), False)
    owner_rows = owner.reshape(32, 128)
    cell_rows = cell.reshape(32, 128)
    slot = pl.pallas_call(
        rank_kernel,
        out_shape=shape((32, 128), jnp.int32),
        in_specs=[HBM] * 2,
        out_specs=VMEM,
        scratch_shapes=[
            pltpu.VMEM((32, 128), jnp.int32),
            pltpu.VMEM((32, 128), jnp.int32),
            pltpu.SemaphoreType.DMA((2,)),
        ],
        compiler_params=params(60),
        cost_estimate=cost(3),
        name="rank",
    )(owner_rows, cell_rows)
    membrane_force, send = pl.pallas_call(
        pack_kernel,
        out_shape=(shape((3, 2, 16, 128), F32), shape((DEVICES, 1, 7 * SLOTS), F32)),
        in_specs=[HBM] * 3 + [VMEM] * 2 + [HBM] * 3 + [VMEM],
        out_specs=(VMEM, VMEM),
        scratch_shapes=[
            pltpu.SMEM((2,), F32),
            pltpu.SMEM((2,), F32),
            pltpu.VMEM((3, 2, 16, 128), F32),
            pltpu.VMEM((32, 128), jnp.int32),
            pltpu.VMEM((32, 128), jnp.int32),
            pltpu.VMEM((3, 2, 32, 128), F32),
            pltpu.VMEM((3, 2, 32, 128), F32),
            pltpu.VMEM((15 * SLOTS, 4096), BF16),
            pltpu.VMEM((DEVICES, 4096), BF16),
            pltpu.SemaphoreType.DMA((6,)),
        ],
        compiler_params=params(60),
        cost_estimate=cost(5),
        name="pack",
    )(
        tension, bending, displacement, before, after, offset, owner_rows, cell_rows, slot
    )
    own = lax.all_to_all(send, ("ves", "shard"), split_axis=0, concat_axis=0, tiled=True)
    own = own.reshape(DEVICES, 7 * SLOTS)
    below = passed_along(own, 1)
    above = passed_along(own, -1)
    held = spread_own(own)
    first, field, moved, up_0, down_0 = first_half(below, above, held, populations)
    up_0, down_0 = passed_along(up_0, 1), passed_along(down_0, -1)
    field, moved, up_1, down_1 = second_half(below, above, held, first, populations, field, moved)
    up_1, down_1 = passed_along(up_1, 1), passed_along(down_1, -1)
    force_field = field.reshape(2, 3, WIDTH, WIDTH)
    moved = place([0], [up_0], [down_0], moved)
    moved = place([HALF], [up_1], [down_1], moved)
    return (membrane_force, force_field, moved)


def solution(mesh):
    return jax.shard_map(
        on_device,
        mesh=mesh,
        in_specs=(
            P(None, "ves", "shard", None),
            P("ves"),
            P("ves"),
            P(None, "ves", "shard", None),
            P("ves", "shard", None),
            P("ves", "shard", None),
            P(("ves", "shard"), None, None, None),
        ),
        out_specs=(
            P(None, "ves", "shard", None),
            P(("ves", "shard"), None, None, None),
            P(("ves", "shard"), None, None, None),
        ),
        check_vma=False,
    )
```

```python
import functools
import math

import jax
import jax.numpy as jnp
from jax import lax
from jax.experimental import pallas as pl
from jax.experimental.pallas import tpu as pltpu
from jax.sharding import PartitionSpec as P

relax_time = 0.8
velocity_x = [0, 1, -1, 0, 0, 0, 1, -1, 0, 0, 0, 1, -1, 0, 0, 1, 1, -1, -1]
velocity_y = [0, 0, 0, 1, -1, 0, 0, 0, 1, -1, 0, 0, 0, 1, -1, 1, -1, 1, -1]
velocity_z = [1, 1, 1, 1, 1, -1, -1, -1, -1, -1, 0, 0, 0, 0, 0, 0, 0, 0, 0]
pairs = [(0, 5), (1, 7), (2, 6), (3, 9), (4, 8), (11, 12), (13, 14), (15, 18), (16, 17)]
SLOTS = 64
DEVICES = 128
WIDTH = 256
F32 = jnp.float32
BF16 = jnp.bfloat16
VMEM = pl.BlockSpec(memory_space=pltpu.VMEM)
SMEM = pl.BlockSpec(memory_space=pltpu.SMEM)
ANY = pl.BlockSpec(memory_space=pl.ANY)
HBM = pl.BlockSpec(memory_space=pltpu.HBM)
CHUNKS = (128, 128)
EVERY = tuple(range(16))
NT = (((1,), (1,)), ((), ()))


def iota(shape, dim):
    return lax.broadcasted_iota(jnp.int32, shape, dim)


def fetch(moves, sem):
    copies = [pltpu.make_async_copy(*move, sem.at[n]) for n, move in enumerate(moves)]
    for copy in copies:
        copy.start()
    for copy in copies:
        copy.wait()


def rank_kernel(owner_from, cell_from, slot_ref, owner_ref, cell_ref, sem):
    fetch(((owner_from, owner_ref), (cell_from, cell_ref)), sem)
    classes = 2 * DEVICES
    before = jnp.where(iota((256, 512), 0) < iota((256, 512), 1), 1.0, 0.0)
    before = before.astype(BF16)
    label = owner_ref[...] + DEVICES * (cell_ref[...] >> 16)
    carry = jnp.zeros((classes, 256), F32)
    rows = iota((classes, 128), 0)
    for k in range(label.shape[0] // 2):
        member = jnp.concatenate(
            [jnp.where(rows == label[2 * k + s : 2 * k + s + 1], 1.0, 0.0) for s in range(2)], 1
        )
        count = jnp.dot(member.astype(BF16), before, preferred_element_type=F32)
        place = jnp.sum(member * (count[:, :256] + carry), 0, keepdims=True)
        carry = carry + count[:, 256:]
        for s in range(2):
            slot_ref[2 * k + s : 2 * k + s + 1, :] = place[:, 128 * s : 128 * s + 128].astype(
                jnp.int32
            )
    place = slot_ref[...]
    slot_ref[...] = jnp.where(label < DEVICES, place, SLOTS - 1 - place)


def pack_kernel(
    tension_from,
    bending_from,
    displacement_from,
    before_ref,
    after_ref,
    offset_from,
    owner_from,
    cell_from,
    slot_ref,
    force_ref,
    send_ref,
    tension_ref,
    bending_ref,
    offset_ref,
    owner_ref,
    cell_ref,
    padded_ref,
    first_ref,
    left_ref,
    right_ref,
    sem,
):
    rows = displacement_from.shape[2]
    fetch(
        (
            (tension_from, tension_ref),
            (bending_from, bending_ref),
            (offset_from, offset_ref),
            (owner_from, owner_ref),
            (cell_from, cell_ref),
            (displacement_from, padded_ref.at[:, :, pl.ds(8, rows)]),
        ),
        sem,
    )
    here = lax.axis_index("shard")
    inside = ((here > 0).astype(F32), (here < lax.axis_size("shard") - 1).astype(F32))
    padded_ref[:, :, 6:8] = before_ref[...]
    padded_ref[:, :, 8 + rows : 10 + rows] = after_ref[...]

    def laplacian(ref, c, v, start, count):
        center = ref[c, v, start : start + count]
        return (
            ref[c, v, start + 1 : start + 1 + count]
            + ref[c, v, start - 1 : start - 1 + count]
            + pltpu.roll(center, 1, 1)
            + pltpu.roll(center, 127, 1)
            - 4.0 * center
        )

    for c in range(3):
        for v in range(2):
            first_ref[c, v, 8 : 8 + rows] = laplacian(padded_ref, c, v, 8, rows)
            first_ref[c, v, 7:8] = laplacian(padded_ref, c, v, 7, 1) * inside[0]
            first_ref[c, v, 8 + rows : 9 + rows] = (
                laplacian(padded_ref, c, v, 8 + rows, 1) * inside[1]
            )
            force_ref[c, v] = tension_ref[v] * first_ref[
                c, v, 8 : 8 + rows
            ] - bending_ref[v] * laplacian(first_ref, c, v, 8, rows)

    parts = []
    for ref in (force_ref, offset_ref):
        for c in range(3):
            value = ref[c].reshape(2 * rows, 128)
            high = value.astype(BF16).astype(F32)
            parts += [high, value - high]
    cell = cell_ref[...]
    parts += [
        ((cell >> 8) & 255).astype(F32),
        (cell & 255).astype(F32),
        (cell >> 16).astype(F32) + 1.0,
    ]
    slots = iota((SLOTS, 128), 0)
    owners = iota((DEVICES, 128), 0)
    for row in range(2 * rows):
        lanes = pl.ds(row * 128, 128)
        here = slots == slot_ref[row : row + 1]
        for n, part in enumerate(parts):
            left_ref[n * SLOTS : (n + 1) * SLOTS, lanes] = jnp.where(
                here, part[row : row + 1], 0.0
            ).astype(BF16)
        right_ref[:, lanes] = jnp.where(owners == owner_ref[row : row + 1], 1.0, 0.0).astype(BF16)
    placed = lax.dot_general(left_ref[...], right_ref[...], NT, preferred_element_type=F32)
    group = [placed[n * SLOTS : (n + 1) * SLOTS] for n in range(len(parts))]
    values = [group[2 * n] + group[2 * n + 1] for n in range(6)]
    code = jnp.where(
        group[14] > 0.5, (group[14] - 1.0) * 65536.0 + group[12] * 256.0 + group[13] + 1.0, 0.0
    )
    send_ref[:, 0, :] = jnp.concatenate(values + [code], 0).T


GROUP = 8


def spread_source(points_ref, targets, blocks, entry, total, buffers, add, tall=768):
    rows16 = iota((16, 128), 0)
    rows = 16 * len(blocks)

    def windows(base, weights):
        low = base & 15
        pieces = []
        for shift in (0, 16):
            near = rows16 + shift - low
            piece = jnp.zeros((16, 128), F32)
            for tap in range(4):
                piece = jnp.where(near == tap, weights[tap], piece)
            pieces.append(piece)
        return pieces

    def build(index, left_ref, right_ref):
        begin, weigh, _ = entry(jnp.minimum(index, total - 1))
        used = (index < total).astype(F32)

        def item(n):
            return points_ref[pl.ds(pl.multiple_of(n * SLOTS + begin, GROUP), GROUP), :]

        cell = item(6).astype(jnp.int32) - 1
        plane = cell >> 16
        base_x = (((cell >> 8) & 255) - 1) & 255
        base_y = ((cell & 255) - 1) & 255
        taps = []
        for c in range(3):
            angle = item(3 + c) * (0.5 * math.pi)
            cosine, sine = 0.25 * jnp.cos(angle), 0.25 * jnp.sin(angle)
            taps.append([0.25 - sine, 0.25 + cosine, 0.25 + sine, 0.25 - cosine])
        scaled = []
        for weight_z in weigh(plane, taps[2]):
            weight_z = weight_z * used
            scaled += [item(c) * weight_z for c in range(3)]
        high_x = (base_x >> 4).astype(F32)
        high_y = (base_y >> 4).astype(F32)
        zero = jnp.zeros((16, 128), BF16)

        def slice_of(r):
            lanes = pl.ds(r * 128, 128)

            def at(value):
                return jnp.broadcast_to(value[r : r + 1], (16, 128))

            near_x = windows(at(base_x), [at(t) for t in taps[0]])
            near_y = [p.astype(BF16) for p in windows(at(base_y), [at(t) for t in taps[1]])]
            left = [[(at(s) * piece).astype(BF16) for piece in near_x] for s in scaled]
            block_x = at(high_x).astype(BF16)
            block_y = at(high_y).astype(BF16)
            is_x = [block_x == jnp.asarray(g, BF16) for g in range(16)]
            is_y = [block_y == jnp.asarray(g, BF16) for g in range(16)]
            for g in range(16):
                right_ref[16 * g : 16 * g + 16, lanes] = jnp.where(
                    is_y[g], near_y[0], jnp.where(is_y[g - 1], near_y[1], zero)
                )
            for k, g in enumerate(blocks):
                for n, (low, high) in enumerate(left):
                    left_ref[pl.ds(rows * n + 16 * k, 16), lanes] = jnp.where(
                        is_x[g], low, jnp.where(is_x[g - 1], high, zero)
                    )

        return slice_of

    height = 3 * rows * targets
    parts = max(1, (height + tall // 2) // tall)

    def product(index, left_ref, right_ref, n):
        first = 0 if targets == 2 else 3 * rows * entry(jnp.minimum(index, total - 1))[2]
        low = tall * n
        high = height if n == parts - 1 else low + tall
        add(
            low if targets == 2 else pl.multiple_of(first + low, 8),
            high - low,
            lax.dot_general(
                left_ref[low:high], right_ref[...], NT, preferred_element_type=F32
            ),
        )

    (left_0, right_0), (left_1, right_1) = buffers

    def both(left_a, right_a, index, left_b, right_b):
        slice_of = build(index, left_b, right_b)
        done = 0
        for n in range(parts):
            product(index - 1, left_a, right_a, n)
            while done * parts < (n + 1) * GROUP and done < GROUP:
                slice_of(done)
                done += 1

    @pl.when(total > 0)
    def _():
        slice_of = build(0, left_0, right_0)
        for r in range(GROUP):
            slice_of(r)

        @pl.loop(0, (total + 1) >> 1)
        def _(turn):
            both(left_0, right_0, 2 * turn + 1, left_1, right_1)
            both(left_1, right_1, 2 * turn + 2, left_0, right_0)


def filled(points_ref, begin):
    code = points_ref[begin + 6 * SLOTS : begin + 7 * SLOTS, :]
    slot = iota(code.shape, 0).astype(F32)
    most = jnp.max(jnp.where((code > 0.5) & (code < 65536.5), slot + 1.0, 0.0))
    least = jnp.min(jnp.where(code > 65536.5, slot, float(SLOTS)))
    low = (most.astype(jnp.int32) + GROUP - 1) // GROUP
    return low, least.astype(jnp.int32) // GROUP


def weights_at(source, targets):
    def weigh(plane, taps):
        found = []
        for target in targets:
            pair = []
            for from_plane in range(2):
                reach = target - from_plane - 2 * source
                pair.append(taps[reach + 1] if -1 <= reach <= 2 else jnp.zeros_like(taps[0]))
            found.append(jnp.where(plane == 0, *pair))
        return found

    return weigh


def spread_own_points(own_ref, blocks, points_ref, buffers, add):
    points_ref[0 : 7 * SLOTS] = own_ref[...].T
    low, high = filled(points_ref, 0)
    high = jnp.maximum(low, high)

    def entry(index):
        step = jnp.where(index < low, index, high + index - low)
        return step * GROUP, weights_at(0, (0, 1)), 0

    total = low + SLOTS // GROUP - high
    spread_source(points_ref, 2, blocks, entry, total, buffers, add, 768)


def spread_near_points(below_ref, above_ref, blocks, points_ref, buffers, add):
    points_ref[0 : 7 * SLOTS] = below_ref[...].T
    points_ref[7 * SLOTS : 14 * SLOTS] = above_ref[...].T
    low, high = filled(points_ref, 0)
    low_above, _ = filled(points_ref, 7 * SLOTS)

    def entry(index):
        return (high + index) * GROUP, weights_at(-1, (0, 1)), 0

    spread_source(points_ref, 2, blocks, entry, SLOTS // GROUP - high, buffers, add)
    count = jnp.minimum(low, high)

    def entry_of_one(index):
        above = index >= count
        step = jnp.where(above, index - count, index)

        def weigh(plane, taps):
            return [jnp.where(plane == 0, jnp.where(above, taps[0], taps[3]), 0.0)]

        return (
            jnp.where(above, 7 * SLOTS, 0) + step * GROUP,
            weigh,
            jnp.where(above, 1, 0),
        )

    spread_source(points_ref, 1, blocks, entry_of_one, count + low_above, buffers, add)


def spread_scratch(blocks):
    return [pltpu.VMEM((14 * SLOTS, 128), F32)] + [
        pltpu.VMEM((96 * len(blocks), 128 * GROUP), BF16),
        pltpu.VMEM((256, 128 * GROUP), BF16),
    ] * 2


def spread_own_kernel(own_ref, field_ref, points_ref, left_0, right_0, left_1, right_1):
    field_ref[...] = jnp.zeros_like(field_ref)

    def add(first, count, value):
        field_ref[pl.ds(first, count)] += value

    buffers = ((left_0, right_0), (left_1, right_1))
    spread_own_points(own_ref, EVERY, points_ref, buffers, add)


def spread_own(own):
    return pl.pallas_call(
        spread_own_kernel,
        out_shape=jax.ShapeDtypeStruct((6 * WIDTH, WIDTH), F32),
        in_specs=[VMEM],
        out_specs=VMEM,
        scratch_shapes=spread_scratch(EVERY),
        compiler_params=params(14),
        cost_estimate=cost(8),
        name="spread_own",
    )(own)


def signed(item, vector):
    total = None
    for sign, value in zip((velocity_x[item], velocity_y[item], velocity_z[item]), vector):
        if sign:
            value = value if sign > 0 else -value
            total = value if total is None else total + value
    return total


def post_collision(current, push):
    density = current[0]
    for item in range(1, 19):
        density = density + current[item]
    moment = []
    for table in (velocity_x, velocity_y, velocity_z):
        plus = [current[i] for i in range(19) if table[i] > 0]
        minus = [current[i] for i in range(19) if table[i] < 0]
        moment.append(functools.reduce(jnp.add, plus) - functools.reduce(jnp.add, minus))
    inverse = 1.0 / density
    rate = 1.0 / relax_time
    half = 1.0 - 0.5 * rate
    flux = [m + 0.5 * f for m, f in zip(moment, push)]
    flow = [j * inverse for j in flux]
    rest = rate * density
    for u, j, f in zip(flow, flux, push):
        rest = rest - u * ((1.5 * rate) * j + (3.0 * half) * f)
    linear = [(3.0 * rate) * j + (3.0 * half) * f for j, f in zip(flux, push)]
    square = [(4.5 * rate) * j + (9.0 * half) * f for j, f in zip(flux, push)]
    result = [None] * 19
    result[10] = (1.0 - rate) * current[10] + (1.0 / 3) * rest
    for one, other in pairs:
        weight = 1.0 / 18 if one in (0, 11, 13) else 1.0 / 36
        even = weight * (rest + signed(one, flow) * signed(one, square))
        odd = weight * signed(one, linear)
        result[one] = (1.0 - rate) * current[one] + (even + odd)
        result[other] = (1.0 - rate) * current[other] + (even - odd)
    return result


def row_loads(start, rows, moves, sem):
    spans = [(start - 8, rows + 16, 0)]
    if start == 0:
        spans = [(WIDTH - 8, 8, 0), (0, rows + 8, 8)]
    elif start + rows == WIDTH:
        spans = [(start - 8, rows + 8, 0), (0, 8, rows + 8)]
    loads = []
    for z in range(2):
        group = []
        for n, (source, target) in enumerate(moves):
            for k, (first, count, place) in enumerate(spans):
                group.append(
                    pltpu.make_async_copy(
                        source.at[z, :, pl.ds(first, count)],
                        target.at[z, :, pl.ds(place, count)],
                        sem.at[z, n, k],
                    )
                )
        loads.append(group)
    for copy in loads[0] + loads[1]:
        copy.start()
    return loads


def collide_rows(
    start, rows, loads, current_ref, push_of, moved_ref, up_ref, down_ref, out_ref, carry_ref, out_sem
):
    stores = []
    row = iota((8, WIDTH), 0)
    for z in range(2):
        for copy in loads[z]:
            copy.wait()

        @pl.loop(0, rows // 8 + 2, unroll=6)
        def _(step):
            here = pl.multiple_of(step * 8, 8)
            now = pl.multiple_of(step * 8 + 8, 8)
            current = [current_ref[z, i, pl.ds(here, 8), :] for i in range(19)]
            result = post_collision(current, push_of(z, step))
            slot = 0
            for i in range(19):
                value = result[i]
                if velocity_y[i]:
                    value = pltpu.roll(value, velocity_y[i] % WIDTH, 1)
                if velocity_x[i] == 0:
                    out_ref[z, i, pl.ds(now, 8), :] = value
                    continue
                value = pltpu.roll(value, velocity_x[i] % 8, 0)
                old = carry_ref[slot]
                carry_ref[slot] = value
                slot += 1
                if velocity_x[i] > 0:
                    out_ref[z, i, pl.ds(now, 8), :] = jnp.where(row == 0, old, value)
                else:
                    out_ref[z, i, pl.ds(here, 8), :] = jnp.where(row == 7, value, old)

        within = pl.ds(start, rows)
        for n, (low, high, place) in enumerate(
            (
                (0, 5, moved_ref.at[1, 0:5, within] if z == 0 else up_ref),
                (5, 10, moved_ref.at[0, 5:10, within] if z == 1 else down_ref),
                (10, 19, moved_ref.at[z, 10:19, within]),
            )
        ):
            copy = pltpu.make_async_copy(
                out_ref.at[z, low:high, pl.ds(16, rows)], place, out_sem.at[z, n]
            )
            copy.start()
            stores.append(copy)
    for copy in stores:
        copy.wait()


def collide_scratch(rows):
    return [
        pltpu.VMEM((2, 19, rows + 16, WIDTH), F32),
        pltpu.VMEM((2, 19, rows + 24, WIDTH), F32),
        pltpu.VMEM((10, 8, WIDTH), F32),
        pltpu.SemaphoreType.DMA((2, 2, 2)),
        pltpu.SemaphoreType.DMA((2, 3)),
    ]


def collide_shapes(rows):
    return (
        jax.ShapeDtypeStruct((2, 19, WIDTH, WIDTH), F32),
        jax.ShapeDtypeStruct((5, rows, WIDTH), F32),
        jax.ShapeDtypeStruct((5, rows, WIDTH), F32),
    )


def collide_kernel(
    start,
    rows,
    populations_ref,
    field_ref,
    held_ref,
    moved_ref,
    up_ref,
    down_ref,
    push_ref,
    current_ref,
    out_ref,
    carry_ref,
    in_sem,
    out_sem,
):
    loads = row_loads(
        start, rows, ((populations_ref, current_ref), (field_ref, push_ref)), in_sem
    )

    def push_of(z, step):
        return [push_ref[z, c, pl.ds(pl.multiple_of(step * 8, 8), 8), :] for c in range(3)]

    collide_rows(
        start,
        rows,
        loads,
        current_ref,
        push_of,
        moved_ref,
        up_ref,
        down_ref,
        out_ref,
        carry_ref,
        out_sem,
    )


def collide(start, rows, populations, field, held):
    return pl.pallas_call(
        functools.partial(collide_kernel, start, rows),
        out_shape=collide_shapes(rows),
        in_specs=[HBM, HBM, ANY],
        out_specs=(ANY, VMEM, VMEM),
        scratch_shapes=[pltpu.VMEM((2, 3, rows + 16, WIDTH), F32)] + collide_scratch(rows),
        input_output_aliases={2: 0},
        compiler_params=params(50),
        cost_estimate=cost(9),
        name="collide",
    )(populations, field, held)


def spread_near_kernel(
    rows,
    below_ref,
    above_ref,
    held_ref,
    populations_ref,
    field_to,
    moved_ref,
    up_ref,
    down_ref,
    field_ref,
    points_ref,
    left_0,
    right_0,
    left_1,
    right_1,
    field_sem,
    current_ref,
    out_ref,
    carry_ref,
    in_sem,
    out_sem,
):
    loads = row_loads(0, rows, ((populations_ref, current_ref),), in_sem)

    def add(first, count, value):
        field_ref[pl.ds(first, count)] += value

    buffers = ((left_0, right_0), (left_1, right_1))
    field_ref[...] = held_ref[...]
    spread_near_points(below_ref, above_ref, EVERY, points_ref, buffers, add)
    store = pltpu.make_async_copy(field_ref, field_to, field_sem)
    store.start()

    def push_of(z, step):
        place = (step * 8 + WIDTH - 8) & (WIDTH - 1)
        return [
            field_ref[pl.ds(pl.multiple_of((3 * z + c) * WIDTH + place, 8), 8), :]
            for c in range(3)
        ]

    collide_rows(
        0,
        rows,
        loads,
        current_ref,
        push_of,
        moved_ref,
        up_ref,
        down_ref,
        out_ref,
        carry_ref,
        out_sem,
    )
    store.wait()


def spread_near(rows, below, above, field, populations):
    return pl.pallas_call(
        functools.partial(spread_near_kernel, rows),
        out_shape=(jax.ShapeDtypeStruct((1536, WIDTH), F32),) + collide_shapes(rows),
        in_specs=[VMEM] * 3 + [HBM],
        out_specs=(HBM, ANY, VMEM, VMEM),
        scratch_shapes=[pltpu.VMEM((1536, WIDTH), F32)]
        + spread_scratch(EVERY)
        + [pltpu.SemaphoreType.DMA]
        + collide_scratch(rows),
        compiler_params=params(50),
        cost_estimate=cost(18),
        name="spread_near",
    )(below, above, field, populations)


def place_kernel(starts, *refs):
    count = len(starts)
    ups, downs = refs[:count], refs[count : 2 * count]
    moved_ref, sem = refs[2 * count + 1 :]
    copies = []
    for n, start in enumerate(starts):
        within = pl.ds(start, ups[n].shape[1])
        copies += [
            pltpu.make_async_copy(ups[n], moved_ref.at[0, 0:5, within], sem.at[0, n]),
            pltpu.make_async_copy(downs[n], moved_ref.at[1, 5:10, within], sem.at[1, n]),
        ]
    for copy in copies:
        copy.start()
    for copy in copies:
        copy.wait()


def place(starts, ups, downs, moved):
    count = len(starts)
    return pl.pallas_call(
        functools.partial(place_kernel, starts),
        out_shape=jax.ShapeDtypeStruct(moved.shape, F32),
        in_specs=[VMEM] * (2 * count) + [ANY],
        out_specs=ANY,
        scratch_shapes=[pltpu.SemaphoreType.DMA((2, count))],
        input_output_aliases={2 * count: 0},
        compiler_params=params(8),
        cost_estimate=cost(1),
        name="place",
    )(*ups, *downs, moved)


def passed_along(value, steps, axis=("ves", "shard"), wrap=True):
    count = math.prod(lax.axis_size(a) for a in axis)
    return lax.ppermute(
        value,
        axis,
        [(i, (i + steps) % count) for i in range(count) if wrap or 0 <= i + steps < count],
    )


def cost(microseconds):
    return pl.CostEstimate(
        flops=microseconds * 10**9, bytes_accessed=microseconds * 10**6, transcendentals=0
    )


def params(megabytes):
    return pltpu.CompilerParams(vmem_limit_bytes=megabytes * 1024 * 1024)


def on_device(displacement, tension, bending, offset, owner, cell, populations):
    shape = jax.ShapeDtypeStruct
    before = passed_along(displacement[:, :, -2:], 1, ("shard",), False)
    after = passed_along(displacement[:, :, :2], -1, ("shard",), False)
    owner_rows = owner.reshape(32, 128)
    cell_rows = cell.reshape(32, 128)
    slot = pl.pallas_call(
        rank_kernel,
        out_shape=shape((32, 128), jnp.int32),
        in_specs=[HBM] * 2,
        out_specs=VMEM,
        scratch_shapes=[
            pltpu.VMEM((32, 128), jnp.int32),
            pltpu.VMEM((32, 128), jnp.int32),
            pltpu.SemaphoreType.DMA((2,)),
        ],
        compiler_params=params(60),
        cost_estimate=cost(3),
        name="rank",
    )(owner_rows, cell_rows)
    membrane_force, send = pl.pallas_call(
        pack_kernel,
        out_shape=(shape((3, 2, 16, 128), F32), shape((DEVICES, 1, 7 * SLOTS), F32)),
        in_specs=[HBM] * 3 + [VMEM] * 2 + [HBM] * 3 + [VMEM],
        out_specs=(VMEM, VMEM),
        scratch_shapes=[
            pltpu.SMEM((2,), F32),
            pltpu.SMEM((2,), F32),
            pltpu.VMEM((3, 2, 16, 128), F32),
            pltpu.VMEM((32, 128), jnp.int32),
            pltpu.VMEM((32, 128), jnp.int32),
            pltpu.VMEM((3, 2, 32, 128), F32),
            pltpu.VMEM((3, 2, 32, 128), F32),
            pltpu.VMEM((15 * SLOTS, 4096), BF16),
            pltpu.VMEM((DEVICES, 4096), BF16),
            pltpu.SemaphoreType.DMA((6,)),
        ],
        compiler_params=params(60),
        cost_estimate=cost(5),
        name="pack",
    )(
        tension, bending, displacement, before, after, offset, owner_rows, cell_rows, slot
    )
    own = lax.all_to_all(send, ("ves", "shard"), split_axis=0, concat_axis=0, tiled=True)
    own = own.reshape(DEVICES, 7 * SLOTS)
    below = passed_along(own, 1)
    above = passed_along(own, -1)
    start = CHUNKS[0]
    field, moved, up, down = spread_near(start, below, above, spread_own(own), populations)
    force_field = field.reshape(2, 3, WIDTH, WIDTH)
    ups, downs, starts = [passed_along(up, 1)], [passed_along(down, -1)], [0]
    for rows in CHUNKS[1:]:
        moved, up, down = collide(start, rows, populations, force_field, moved)
        ups.append(passed_along(up, 1))
        downs.append(passed_along(down, -1))
        starts.append(start)
        start += rows
    moved = place(starts[:-1], ups[:-1], downs[:-1], moved)
    moved = place(starts[-1:], ups[-1:], downs[-1:], moved)
    return (membrane_force, force_field, moved)


def solution(mesh):
    return jax.shard_map(
        on_device,
        mesh=mesh,
        in_specs=(
            P(None, "ves", "shard", None),
            P("ves"),
            P("ves"),
            P(None, "ves", "shard", None),
            P("ves", "shard", None),
            P("ves", "shard", None),
            P(("ves", "shard"), None, None, None),
        ),
        out_specs=(
            P(None, "ves", "shard", None),
            P(("ves", "shard"), None, None, None),
            P(("ves", "shard"), None, None, None),
        ),
        check_vma=False,
    )
```

```python
import functools
import math

import jax
import jax.numpy as jnp
from jax import lax
from jax.experimental import pallas as pl
from jax.experimental.pallas import tpu as pltpu
from jax.sharding import PartitionSpec as P

relax_time = 0.8
velocity_x = [0, 1, -1, 0, 0, 0, 1, -1, 0, 0, 0, 1, -1, 0, 0, 1, 1, -1, -1]
velocity_y = [0, 0, 0, 1, -1, 0, 0, 0, 1, -1, 0, 0, 0, 1, -1, 1, -1, 1, -1]
velocity_z = [1, 1, 1, 1, 1, -1, -1, -1, -1, -1, 0, 0, 0, 0, 0, 0, 0, 0, 0]
pairs = [(0, 5), (1, 7), (2, 6), (3, 9), (4, 8), (11, 12), (13, 14), (15, 18), (16, 17)]
SLOTS = 64
DEVICES = 128
WIDTH = 256
F32 = jnp.float32
BF16 = jnp.bfloat16
VMEM = pl.BlockSpec(memory_space=pltpu.VMEM)
SMEM = pl.BlockSpec(memory_space=pltpu.SMEM)
ANY = pl.BlockSpec(memory_space=pl.ANY)
HBM = pl.BlockSpec(memory_space=pltpu.HBM)
CHUNKS = (128, 128)
EVERY = tuple(range(16))
NT = (((1,), (1,)), ((), ()))


def iota(shape, dim):
    return lax.broadcasted_iota(jnp.int32, shape, dim)


def fetch(moves, sem):
    copies = [pltpu.make_async_copy(*move, sem.at[n]) for n, move in enumerate(moves)]
    for copy in copies:
        copy.start()
    for copy in copies:
        copy.wait()


def rank_kernel(owner_from, cell_from, slot_ref, owner_ref, cell_ref, sem):
    fetch(((owner_from, owner_ref), (cell_from, cell_ref)), sem)
    classes = 2 * DEVICES
    before = jnp.where(iota((256, 512), 0) < iota((256, 512), 1), 1.0, 0.0)
    before = before.astype(BF16)
    label = owner_ref[...] + DEVICES * (cell_ref[...] >> 16)
    carry = jnp.zeros((classes, 256), F32)
    rows = iota((classes, 128), 0)
    for k in range(label.shape[0] // 2):
        member = jnp.concatenate(
            [jnp.where(rows == label[2 * k + s : 2 * k + s + 1], 1.0, 0.0) for s in range(2)], 1
        )
        count = jnp.dot(member.astype(BF16), before, preferred_element_type=F32)
        place = jnp.sum(member * (count[:, :256] + carry), 0, keepdims=True)
        carry = carry + count[:, 256:]
        for s in range(2):
            slot_ref[2 * k + s : 2 * k + s + 1, :] = place[:, 128 * s : 128 * s + 128].astype(
                jnp.int32
            )
    place = slot_ref[...]
    slot_ref[...] = jnp.where(label < DEVICES, place, SLOTS - 1 - place)


def pack_kernel(
    tension_from,
    bending_from,
    displacement_from,
    before_ref,
    after_ref,
    offset_from,
    owner_from,
    cell_from,
    slot_ref,
    force_ref,
    send_ref,
    tension_ref,
    bending_ref,
    offset_ref,
    owner_ref,
    cell_ref,
    padded_ref,
    first_ref,
    left_ref,
    right_ref,
    sem,
):
    rows = displacement_from.shape[2]
    fetch(
        (
            (tension_from, tension_ref),
            (bending_from, bending_ref),
            (offset_from, offset_ref),
            (owner_from, owner_ref),
            (cell_from, cell_ref),
            (displacement_from, padded_ref.at[:, :, pl.ds(8, rows)]),
        ),
        sem,
    )
    here = lax.axis_index("shard")
    inside = ((here > 0).astype(F32), (here < lax.axis_size("shard") - 1).astype(F32))
    padded_ref[:, :, 6:8] = before_ref[...]
    padded_ref[:, :, 8 + rows : 10 + rows] = after_ref[...]

    def laplacian(ref, c, v, start, count):
        center = ref[c, v, start : start + count]
        return (
            ref[c, v, start + 1 : start + 1 + count]
            + ref[c, v, start - 1 : start - 1 + count]
            + pltpu.roll(center, 1, 1)
            + pltpu.roll(center, 127, 1)
            - 4.0 * center
        )

    for c in range(3):
        for v in range(2):
            first_ref[c, v, 8 : 8 + rows] = laplacian(padded_ref, c, v, 8, rows)
            first_ref[c, v, 7:8] = laplacian(padded_ref, c, v, 7, 1) * inside[0]
            first_ref[c, v, 8 + rows : 9 + rows] = (
                laplacian(padded_ref, c, v, 8 + rows, 1) * inside[1]
            )
            force_ref[c, v] = tension_ref[v] * first_ref[
                c, v, 8 : 8 + rows
            ] - bending_ref[v] * laplacian(first_ref, c, v, 8, rows)

    parts = []
    for ref in (force_ref, offset_ref):
        for c in range(3):
            value = ref[c].reshape(2 * rows, 128)
            high = value.astype(BF16).astype(F32)
            parts += [high, value - high]
    cell = cell_ref[...]
    parts += [
        ((cell >> 8) & 255).astype(F32),
        (cell & 255).astype(F32),
        (cell >> 16).astype(F32) + 1.0,
    ]
    slots = iota((SLOTS, 128), 0)
    owners = iota((DEVICES, 128), 0)
    for row in range(2 * rows):
        lanes = pl.ds(row * 128, 128)
        here = slots == slot_ref[row : row + 1]
        for n, part in enumerate(parts):
            left_ref[n * SLOTS : (n + 1) * SLOTS, lanes] = jnp.where(
                here, part[row : row + 1], 0.0
            ).astype(BF16)
        right_ref[:, lanes] = jnp.where(owners == owner_ref[row : row + 1], 1.0, 0.0).astype(BF16)
    placed = lax.dot_general(left_ref[...], right_ref[...], NT, preferred_element_type=F32)
    group = [placed[n * SLOTS : (n + 1) * SLOTS] for n in range(len(parts))]
    values = [group[2 * n] + group[2 * n + 1] for n in range(6)]
    code = jnp.where(
        group[14] > 0.5, (group[14] - 1.0) * 65536.0 + group[12] * 256.0 + group[13] + 1.0, 0.0
    )
    send_ref[:, 0, :] = jnp.concatenate(values + [code], 0).T


GROUP = 8


def spread_source(points_ref, targets, blocks, entry, total, buffers, add, tall=768):
    rows16 = iota((16, 128), 0)
    rows = 16 * len(blocks)

    def windows(base, weights):
        low = base & 15
        pieces = []
        for shift in (0, 16):
            near = rows16 + shift - low
            piece = jnp.zeros((16, 128), F32)
            for tap in range(4):
                piece = jnp.where(near == tap, weights[tap], piece)
            pieces.append(piece)
        return pieces

    def build(index, left_ref, right_ref):
        begin, weigh, _ = entry(jnp.minimum(index, total - 1))

        def item(n):
            return points_ref[pl.ds(pl.multiple_of(n * SLOTS + begin, GROUP), GROUP), :]

        cell = item(6).astype(jnp.int32) - 1
        plane = cell >> 16
        base_x = (((cell >> 8) & 255) - 1) & 255
        base_y = ((cell & 255) - 1) & 255
        taps = []
        for c in range(3):
            angle = item(3 + c) * (0.5 * math.pi)
            cosine, sine = 0.25 * jnp.cos(angle), 0.25 * jnp.sin(angle)
            taps.append([0.25 - sine, 0.25 + cosine, 0.25 + sine, 0.25 - cosine])
        scaled = []
        for weight_z in weigh(plane, taps[2]):
            scaled += [item(c) * weight_z for c in range(3)]
        high_x = (base_x >> 4).astype(F32)
        high_y = (base_y >> 4).astype(F32)
        zero = jnp.zeros((16, 128), BF16)

        def slice_of(r):
            lanes = pl.ds(r * 128, 128)

            def at(value):
                return jnp.broadcast_to(value[r : r + 1], (16, 128))

            near_x = windows(at(base_x), [at(t) for t in taps[0]])
            near_y = [p.astype(BF16) for p in windows(at(base_y), [at(t) for t in taps[1]])]
            left = [[(at(s) * piece).astype(BF16) for piece in near_x] for s in scaled]
            block_x = at(high_x).astype(BF16)
            block_y = at(high_y).astype(BF16)
            is_x = [block_x == jnp.asarray(g, BF16) for g in range(16)]
            is_y = [block_y == jnp.asarray(g, BF16) for g in range(16)]
            for g in range(16):
                right_ref[16 * g : 16 * g + 16, lanes] = jnp.where(
                    is_y[g], near_y[0], jnp.where(is_y[g - 1], near_y[1], zero)
                )
            for k, g in enumerate(blocks):
                for n, (low, high) in enumerate(left):
                    left_ref[pl.ds(rows * n + 16 * k, 16), lanes] = jnp.where(
                        is_x[g], low, jnp.where(is_x[g - 1], high, zero)
                    )

        return slice_of

    height = 3 * rows * targets
    parts = max(1, (height + tall // 2) // tall)

    def product(index, left_ref, right_ref, n):
        first = 0 if targets == 2 else 3 * rows * entry(jnp.minimum(index, total - 1))[2]
        low = tall * n
        high = height if n == parts - 1 else low + tall
        add(
            low if targets == 2 else pl.multiple_of(first + low, 8),
            high - low,
            lax.dot_general(
                left_ref[low:high], right_ref[...], NT, preferred_element_type=F32
            ),
        )

    (left_0, right_0), (left_1, right_1) = buffers

    def both(left_a, right_a, index, left_b, right_b):
        slice_of = build(index, left_b, right_b)
        done = 0
        for n in range(parts):
            product(index - 1, left_a, right_a, n)
            while done * parts < (n + 1) * GROUP and done < GROUP:
                slice_of(done)
                done += 1

    @pl.when(total > 0)
    def _():
        slice_of = build(0, left_0, right_0)
        for r in range(GROUP):
            slice_of(r)

        @pl.loop(0, total >> 1)
        def _(turn):
            both(left_0, right_0, 2 * turn + 1, left_1, right_1)
            both(left_1, right_1, 2 * turn + 2, left_0, right_0)

        @pl.when((total & 1) == 1)
        def _():
            for n in range(parts):
                product(total - 1, left_0, right_0, n)


def filled(points_ref, begin):
    code = points_ref[begin + 6 * SLOTS : begin + 7 * SLOTS, :]
    slot = iota(code.shape, 0).astype(F32)
    most = jnp.max(jnp.where((code > 0.5) & (code < 65536.5), slot + 1.0, 0.0))
    least = jnp.min(jnp.where(code > 65536.5, slot, float(SLOTS)))
    low = (most.astype(jnp.int32) + GROUP - 1) // GROUP
    return low, least.astype(jnp.int32) // GROUP


def weights_at(source, targets):
    def weigh(plane, taps):
        found = []
        for target in targets:
            pair = []
            for from_plane in range(2):
                reach = target - from_plane - 2 * source
                pair.append(taps[reach + 1] if -1 <= reach <= 2 else jnp.zeros_like(taps[0]))
            found.append(jnp.where(plane == 0, *pair))
        return found

    return weigh


def spread_own_points(own_ref, blocks, points_ref, buffers, add):
    points_ref[0 : 7 * SLOTS] = own_ref[...].T
    low, high = filled(points_ref, 0)
    high = jnp.maximum(low, high)

    def entry(index):
        step = jnp.where(index < low, index, high + index - low)
        return step * GROUP, weights_at(0, (0, 1)), 0

    total = low + SLOTS // GROUP - high
    spread_source(points_ref, 2, blocks, entry, total, buffers, add, 768)


def spread_near_points(below_ref, above_ref, blocks, points_ref, buffers, add):
    points_ref[0 : 7 * SLOTS] = below_ref[...].T
    points_ref[7 * SLOTS : 14 * SLOTS] = above_ref[...].T
    low, high = filled(points_ref, 0)
    low_above, _ = filled(points_ref, 7 * SLOTS)

    def entry(index):
        return (high + index) * GROUP, weights_at(-1, (0, 1)), 0

    spread_source(points_ref, 2, blocks, entry, SLOTS // GROUP - high, buffers, add)
    count = jnp.minimum(low, high)

    def entry_of_one(index):
        above = index >= count
        step = jnp.where(above, index - count, index)

        def weigh(plane, taps):
            return [jnp.where(plane == 0, jnp.where(above, taps[0], taps[3]), 0.0)]

        return (
            jnp.where(above, 7 * SLOTS, 0) + step * GROUP,
            weigh,
            jnp.where(above, 1, 0),
        )

    spread_source(points_ref, 1, blocks, entry_of_one, count + low_above, buffers, add)


def spread_scratch(blocks):
    return [pltpu.VMEM((14 * SLOTS, 128), F32)] + [
        pltpu.VMEM((96 * len(blocks), 128 * GROUP), BF16),
        pltpu.VMEM((256, 128 * GROUP), BF16),
    ] * 2


def spread_own_kernel(own_ref, field_ref, points_ref, left_0, right_0, left_1, right_1):
    field_ref[...] = jnp.zeros_like(field_ref)

    def add(first, count, value):
        field_ref[pl.ds(first, count)] += value

    buffers = ((left_0, right_0), (left_1, right_1))
    spread_own_points(own_ref, EVERY, points_ref, buffers, add)


def spread_own(own):
    return pl.pallas_call(
        spread_own_kernel,
        out_shape=jax.ShapeDtypeStruct((6 * WIDTH, WIDTH), F32),
        in_specs=[VMEM],
        out_specs=VMEM,
        scratch_shapes=spread_scratch(EVERY),
        compiler_params=params(14),
        cost_estimate=cost(8),
        name="spread_own",
    )(own)


def signed(item, vector):
    total = None
    for sign, value in zip((velocity_x[item], velocity_y[item], velocity_z[item]), vector):
        if sign:
            value = value if sign > 0 else -value
            total = value if total is None else total + value
    return total


def post_collision(current, push):
    density = current[0]
    for item in range(1, 19):
        density = density + current[item]
    moment = []
    for table in (velocity_x, velocity_y, velocity_z):
        plus = [current[i] for i in range(19) if table[i] > 0]
        minus = [current[i] for i in range(19) if table[i] < 0]
        moment.append(functools.reduce(jnp.add, plus) - functools.reduce(jnp.add, minus))
    inverse = 1.0 / density
    rate = 1.0 / relax_time
    half = 1.0 - 0.5 * rate
    flux = [m + 0.5 * f for m, f in zip(moment, push)]
    flow = [j * inverse for j in flux]
    rest = rate * density
    for u, j, f in zip(flow, flux, push):
        rest = rest - u * ((1.5 * rate) * j + (3.0 * half) * f)
    linear = [(3.0 * rate) * j + (3.0 * half) * f for j, f in zip(flux, push)]
    square = [(4.5 * rate) * j + (9.0 * half) * f for j, f in zip(flux, push)]
    result = [None] * 19
    result[10] = (1.0 - rate) * current[10] + (1.0 / 3) * rest
    for one, other in pairs:
        weight = 1.0 / 18 if one in (0, 11, 13) else 1.0 / 36
        even = weight * (rest + signed(one, flow) * signed(one, square))
        odd = weight * signed(one, linear)
        result[one] = (1.0 - rate) * current[one] + (even + odd)
        result[other] = (1.0 - rate) * current[other] + (even - odd)
    return result


def row_loads(start, rows, moves, sem):
    spans = [(start - 8, rows + 16, 0)]
    if start == 0:
        spans = [(WIDTH - 8, 8, 0), (0, rows + 8, 8)]
    elif start + rows == WIDTH:
        spans = [(start - 8, rows + 8, 0), (0, 8, rows + 8)]
    loads = []
    for z in range(2):
        group = []
        for n, (source, target) in enumerate(moves):
            for k, (first, count, place) in enumerate(spans):
                group.append(
                    pltpu.make_async_copy(
                        source.at[z, :, pl.ds(first, count)],
                        target.at[z, :, pl.ds(place, count)],
                        sem.at[z, n, k],
                    )
                )
        loads.append(group)
    for copy in loads[0] + loads[1]:
        copy.start()
    return loads


def collide_rows(
    start, rows, loads, current_ref, push_of, moved_ref, up_ref, down_ref, out_ref, carry_ref, out_sem
):
    stores = []
    row = iota((8, WIDTH), 0)
    for z in range(2):
        for copy in loads[z]:
            copy.wait()

        @pl.loop(0, rows // 8 + 2, unroll=6)
        def _(step):
            here = pl.multiple_of(step * 8, 8)
            now = pl.multiple_of(step * 8 + 8, 8)
            current = [current_ref[z, i, pl.ds(here, 8), :] for i in range(19)]
            result = post_collision(current, push_of(z, step))
            slot = 0
            for i in range(19):
                value = result[i]
                if velocity_y[i]:
                    value = pltpu.roll(value, velocity_y[i] % WIDTH, 1)
                if velocity_x[i] == 0:
                    out_ref[z, i, pl.ds(now, 8), :] = value
                    continue
                value = pltpu.roll(value, velocity_x[i] % 8, 0)
                old = carry_ref[slot]
                carry_ref[slot] = value
                slot += 1
                if velocity_x[i] > 0:
                    out_ref[z, i, pl.ds(now, 8), :] = jnp.where(row == 0, old, value)
                else:
                    out_ref[z, i, pl.ds(here, 8), :] = jnp.where(row == 7, value, old)

        within = pl.ds(start, rows)
        for n, (low, high, place) in enumerate(
            (
                (0, 5, moved_ref.at[1, 0:5, within] if z == 0 else up_ref),
                (5, 10, moved_ref.at[0, 5:10, within] if z == 1 else down_ref),
                (10, 19, moved_ref.at[z, 10:19, within]),
            )
        ):
            copy = pltpu.make_async_copy(
                out_ref.at[z, low:high, pl.ds(16, rows)], place, out_sem.at[z, n]
            )
            copy.start()
            stores.append(copy)
    for copy in stores:
        copy.wait()


def collide_scratch(rows):
    return [
        pltpu.VMEM((2, 19, rows + 16, WIDTH), F32),
        pltpu.VMEM((2, 19, rows + 24, WIDTH), F32),
        pltpu.VMEM((10, 8, WIDTH), F32),
        pltpu.SemaphoreType.DMA((2, 2, 2)),
        pltpu.SemaphoreType.DMA((2, 3)),
    ]


def collide_shapes(rows):
    return (
        jax.ShapeDtypeStruct((2, 19, WIDTH, WIDTH), F32),
        jax.ShapeDtypeStruct((5, rows, WIDTH), F32),
        jax.ShapeDtypeStruct((5, rows, WIDTH), F32),
    )


def collide_kernel(
    start,
    rows,
    populations_ref,
    field_ref,
    held_ref,
    moved_ref,
    up_ref,
    down_ref,
    push_ref,
    current_ref,
    out_ref,
    carry_ref,
    in_sem,
    out_sem,
):
    loads = row_loads(
        start, rows, ((populations_ref, current_ref), (field_ref, push_ref)), in_sem
    )

    def push_of(z, step):
        return [push_ref[z, c, pl.ds(pl.multiple_of(step * 8, 8), 8), :] for c in range(3)]

    collide_rows(
        start,
        rows,
        loads,
        current_ref,
        push_of,
        moved_ref,
        up_ref,
        down_ref,
        out_ref,
        carry_ref,
        out_sem,
    )


def collide(start, rows, populations, field, held):
    return pl.pallas_call(
        functools.partial(collide_kernel, start, rows),
        out_shape=collide_shapes(rows),
        in_specs=[HBM, HBM, ANY],
        out_specs=(ANY, VMEM, VMEM),
        scratch_shapes=[pltpu.VMEM((2, 3, rows + 16, WIDTH), F32)] + collide_scratch(rows),
        input_output_aliases={2: 0},
        compiler_params=params(50),
        cost_estimate=cost(9),
        name="collide",
    )(populations, field, held)


def spread_near_kernel(
    rows,
    below_ref,
    above_ref,
    held_ref,
    populations_ref,
    field_to,
    moved_ref,
    up_ref,
    down_ref,
    field_ref,
    points_ref,
    left_0,
    right_0,
    left_1,
    right_1,
    field_sem,
    current_ref,
    out_ref,
    carry_ref,
    in_sem,
    out_sem,
):
    loads = row_loads(0, rows, ((populations_ref, current_ref),), in_sem)

    def add(first, count, value):
        field_ref[pl.ds(first, count)] += value

    buffers = ((left_0, right_0), (left_1, right_1))
    field_ref[...] = held_ref[...]
    spread_near_points(below_ref, above_ref, EVERY, points_ref, buffers, add)
    store = pltpu.make_async_copy(field_ref, field_to, field_sem)
    store.start()

    def push_of(z, step):
        place = (step * 8 + WIDTH - 8) & (WIDTH - 1)
        return [
            field_ref[pl.ds(pl.multiple_of((3 * z + c) * WIDTH + place, 8), 8), :]
            for c in range(3)
        ]

    collide_rows(
        0,
        rows,
        loads,
        current_ref,
        push_of,
        moved_ref,
        up_ref,
        down_ref,
        out_ref,
        carry_ref,
        out_sem,
    )
    store.wait()


def spread_near(rows, below, above, field, populations):
    return pl.pallas_call(
        functools.partial(spread_near_kernel, rows),
        out_shape=(jax.ShapeDtypeStruct((1536, WIDTH), F32),) + collide_shapes(rows),
        in_specs=[VMEM] * 3 + [HBM],
        out_specs=(HBM, ANY, VMEM, VMEM),
        scratch_shapes=[pltpu.VMEM((1536, WIDTH), F32)]
        + spread_scratch(EVERY)
        + [pltpu.SemaphoreType.DMA]
        + collide_scratch(rows),
        compiler_params=params(50),
        cost_estimate=cost(18),
        name="spread_near",
    )(below, above, field, populations)


def place_kernel(starts, *refs):
    count = len(starts)
    ups, downs = refs[:count], refs[count : 2 * count]
    moved_ref, sem = refs[2 * count + 1 :]
    copies = []
    for n, start in enumerate(starts):
        within = pl.ds(start, ups[n].shape[1])
        copies += [
            pltpu.make_async_copy(ups[n], moved_ref.at[0, 0:5, within], sem.at[0, n]),
            pltpu.make_async_copy(downs[n], moved_ref.at[1, 5:10, within], sem.at[1, n]),
        ]
    for copy in copies:
        copy.start()
    for copy in copies:
        copy.wait()


def place(starts, ups, downs, moved):
    count = len(starts)
    return pl.pallas_call(
        functools.partial(place_kernel, starts),
        out_shape=jax.ShapeDtypeStruct(moved.shape, F32),
        in_specs=[VMEM] * (2 * count) + [ANY],
        out_specs=ANY,
        scratch_shapes=[pltpu.SemaphoreType.DMA((2, count))],
        input_output_aliases={2 * count: 0},
        compiler_params=params(8),
        cost_estimate=cost(1),
        name="place",
    )(*ups, *downs, moved)


def passed_along(value, steps, axis=("ves", "shard"), wrap=True):
    count = math.prod(lax.axis_size(a) for a in axis)
    return lax.ppermute(
        value,
        axis,
        [(i, (i + steps) % count) for i in range(count) if wrap or 0 <= i + steps < count],
    )


def cost(microseconds):
    return pl.CostEstimate(
        flops=microseconds * 10**9, bytes_accessed=microseconds * 10**6, transcendentals=0
    )


def params(megabytes):
    return pltpu.CompilerParams(vmem_limit_bytes=megabytes * 1024 * 1024)


def on_device(displacement, tension, bending, offset, owner, cell, populations):
    shape = jax.ShapeDtypeStruct
    before = passed_along(displacement[:, :, -2:], 1, ("shard",), False)
    after = passed_along(displacement[:, :, :2], -1, ("shard",), False)
    owner_rows = owner.reshape(32, 128)
    cell_rows = cell.reshape(32, 128)
    slot = pl.pallas_call(
        rank_kernel,
        out_shape=shape((32, 128), jnp.int32),
        in_specs=[HBM] * 2,
        out_specs=VMEM,
        scratch_shapes=[
            pltpu.VMEM((32, 128), jnp.int32),
            pltpu.VMEM((32, 128), jnp.int32),
            pltpu.SemaphoreType.DMA((2,)),
        ],
        compiler_params=params(60),
        cost_estimate=cost(3),
        name="rank",
    )(owner_rows, cell_rows)
    membrane_force, send = pl.pallas_call(
        pack_kernel,
        out_shape=(shape((3, 2, 16, 128), F32), shape((DEVICES, 1, 7 * SLOTS), F32)),
        in_specs=[HBM] * 3 + [VMEM] * 2 + [HBM] * 3 + [VMEM],
        out_specs=(VMEM, VMEM),
        scratch_shapes=[
            pltpu.SMEM((2,), F32),
            pltpu.SMEM((2,), F32),
            pltpu.VMEM((3, 2, 16, 128), F32),
            pltpu.VMEM((32, 128), jnp.int32),
            pltpu.VMEM((32, 128), jnp.int32),
            pltpu.VMEM((3, 2, 32, 128), F32),
            pltpu.VMEM((3, 2, 32, 128), F32),
            pltpu.VMEM((15 * SLOTS, 4096), BF16),
            pltpu.VMEM((DEVICES, 4096), BF16),
            pltpu.SemaphoreType.DMA((6,)),
        ],
        compiler_params=params(60),
        cost_estimate=cost(5),
        name="pack",
    )(
        tension, bending, displacement, before, after, offset, owner_rows, cell_rows, slot
    )
    own = lax.all_to_all(send, ("ves", "shard"), split_axis=0, concat_axis=0, tiled=True)
    own = own.reshape(DEVICES, 7 * SLOTS)
    below = passed_along(own, 1)
    above = passed_along(own, -1)
    start = CHUNKS[0]
    field, moved, up, down = spread_near(start, below, above, spread_own(own), populations)
    force_field = field.reshape(2, 3, WIDTH, WIDTH)
    ups, downs, starts = [passed_along(up, 1)], [passed_along(down, -1)], [0]
    for rows in CHUNKS[1:]:
        moved, up, down = collide(start, rows, populations, force_field, moved)
        ups.append(passed_along(up, 1))
        downs.append(passed_along(down, -1))
        starts.append(start)
        start += rows
    moved = place(starts[:-1], ups[:-1], downs[:-1], moved)
    moved = place(starts[-1:], ups[-1:], downs[-1:], moved)
    return (membrane_force, force_field, moved)


def solution(mesh):
    return jax.shard_map(
        on_device,
        mesh=mesh,
        in_specs=(
            P(None, "ves", "shard", None),
            P("ves"),
            P("ves"),
            P(None, "ves", "shard", None),
            P("ves", "shard", None),
            P("ves", "shard", None),
            P(("ves", "shard"), None, None, None),
        ),
        out_specs=(
            P(None, "ves", "shard", None),
            P(("ves", "shard"), None, None, None),
            P(("ves", "shard"), None, None, None),
        ),
        check_vma=False,
    )
```

```python
import functools
import math

import jax
import jax.numpy as jnp
from jax import lax
from jax.experimental import pallas as pl
from jax.experimental.pallas import tpu as pltpu
from jax.sharding import PartitionSpec as P

relax_time = 0.8
velocity_x = [0, 1, -1, 0, 0, 0, 1, -1, 0, 0, 0, 1, -1, 0, 0, 1, 1, -1, -1]
velocity_y = [0, 0, 0, 1, -1, 0, 0, 0, 1, -1, 0, 0, 0, 1, -1, 1, -1, 1, -1]
velocity_z = [1, 1, 1, 1, 1, -1, -1, -1, -1, -1, 0, 0, 0, 0, 0, 0, 0, 0, 0]
pairs = [(0, 5), (1, 7), (2, 6), (3, 9), (4, 8), (11, 12), (13, 14), (15, 18), (16, 17)]
SLOTS = 64
DEVICES = 128
WIDTH = 256
F32 = jnp.float32
BF16 = jnp.bfloat16
VMEM = pl.BlockSpec(memory_space=pltpu.VMEM)
SMEM = pl.BlockSpec(memory_space=pltpu.SMEM)
ANY = pl.BlockSpec(memory_space=pl.ANY)
HBM = pl.BlockSpec(memory_space=pltpu.HBM)
CHUNKS = (128, 128)
EVERY = tuple(range(16))
NT = (((1,), (1,)), ((), ()))


def iota(shape, dim):
    return lax.broadcasted_iota(jnp.int32, shape, dim)


def fetch(moves, sem):
    copies = [pltpu.make_async_copy(*move, sem.at[n]) for n, move in enumerate(moves)]
    for copy in copies:
        copy.start()
    for copy in copies:
        copy.wait()


def rank_kernel(owner_from, cell_from, slot_ref, owner_ref, cell_ref, sem):
    fetch(((owner_from, owner_ref), (cell_from, cell_ref)), sem)
    classes = 2 * DEVICES
    before = jnp.where(iota((256, 512), 0) < iota((256, 512), 1), 1.0, 0.0)
    before = before.astype(BF16)
    label = owner_ref[...] + DEVICES * (cell_ref[...] >> 16)
    carry = jnp.zeros((classes, 256), F32)
    rows = iota((classes, 128), 0)
    for k in range(label.shape[0] // 2):
        member = jnp.concatenate(
            [jnp.where(rows == label[2 * k + s : 2 * k + s + 1], 1.0, 0.0) for s in range(2)], 1
        )
        count = jnp.dot(member.astype(BF16), before, preferred_element_type=F32)
        place = jnp.sum(member * (count[:, :256] + carry), 0, keepdims=True)
        carry = carry + count[:, 256:]
        for s in range(2):
            slot_ref[2 * k + s : 2 * k + s + 1, :] = place[:, 128 * s : 128 * s + 128].astype(
                jnp.int32
            )
    place = slot_ref[...]
    slot_ref[...] = jnp.where(label < DEVICES, place, SLOTS - 1 - place)


def pack_kernel(
    tension_from,
    bending_from,
    displacement_from,
    before_ref,
    after_ref,
    offset_from,
    owner_from,
    cell_from,
    slot_ref,
    force_ref,
    send_ref,
    tension_ref,
    bending_ref,
    offset_ref,
    owner_ref,
    cell_ref,
    padded_ref,
    first_ref,
    left_ref,
    right_ref,
    sem,
):
    rows = displacement_from.shape[2]
    fetch(
        (
            (tension_from, tension_ref),
            (bending_from, bending_ref),
            (offset_from, offset_ref),
            (owner_from, owner_ref),
            (cell_from, cell_ref),
            (displacement_from, padded_ref.at[:, :, pl.ds(8, rows)]),
        ),
        sem,
    )
    here = lax.axis_index("shard")
    inside = ((here > 0).astype(F32), (here < lax.axis_size("shard") - 1).astype(F32))
    padded_ref[:, :, 6:8] = before_ref[...]
    padded_ref[:, :, 8 + rows : 10 + rows] = after_ref[...]

    def laplacian(ref, c, v, start, count):
        center = ref[c, v, start : start + count]
        return (
            ref[c, v, start + 1 : start + 1 + count]
            + ref[c, v, start - 1 : start - 1 + count]
            + pltpu.roll(center, 1, 1)
            + pltpu.roll(center, 127, 1)
            - 4.0 * center
        )

    for c in range(3):
        for v in range(2):
            first_ref[c, v, 8 : 8 + rows] = laplacian(padded_ref, c, v, 8, rows)
            first_ref[c, v, 7:8] = laplacian(padded_ref, c, v, 7, 1) * inside[0]
            first_ref[c, v, 8 + rows : 9 + rows] = (
                laplacian(padded_ref, c, v, 8 + rows, 1) * inside[1]
            )
            force_ref[c, v] = tension_ref[v] * first_ref[
                c, v, 8 : 8 + rows
            ] - bending_ref[v] * laplacian(first_ref, c, v, 8, rows)

    parts = []
    for ref in (force_ref, offset_ref):
        for c in range(3):
            value = ref[c].reshape(2 * rows, 128)
            high = value.astype(BF16).astype(F32)
            parts += [high, value - high]
    cell = cell_ref[...]
    parts += [
        ((cell >> 8) & 255).astype(F32),
        (cell & 255).astype(F32),
        (cell >> 16).astype(F32) + 1.0,
    ]
    slots = iota((SLOTS, 128), 0)
    owners = iota((DEVICES, 128), 0)
    for row in range(2 * rows):
        lanes = pl.ds(row * 128, 128)
        here = slots == slot_ref[row : row + 1]
        for n, part in enumerate(parts):
            left_ref[n * SLOTS : (n + 1) * SLOTS, lanes] = jnp.where(
                here, part[row : row + 1], 0.0
            ).astype(BF16)
        right_ref[:, lanes] = jnp.where(owners == owner_ref[row : row + 1], 1.0, 0.0).astype(BF16)
    placed = lax.dot_general(left_ref[...], right_ref[...], NT, preferred_element_type=F32)
    group = [placed[n * SLOTS : (n + 1) * SLOTS] for n in range(len(parts))]
    values = [group[2 * n] + group[2 * n + 1] for n in range(6)]
    code = jnp.where(
        group[14] > 0.5, (group[14] - 1.0) * 65536.0 + group[12] * 256.0 + group[13] + 1.0, 0.0
    )
    send_ref[:, 0, :] = jnp.concatenate(values + [code], 0).T


GROUP = 8


def spread_source(points_ref, targets, blocks, entry, total, buffers, add, tall=768):
    rows16 = iota((16, 128), 0)
    rows = 16 * len(blocks)

    def windows(base, weights):
        low = base & 15
        pieces = []
        for shift in (0, 16):
            near = rows16 + shift - low
            piece = jnp.zeros((16, 128), F32)
            for tap in range(4):
                piece = jnp.where(near == tap, weights[tap], piece)
            pieces.append(piece)
        return pieces

    def build(index, left_ref, right_ref):
        begin, weigh, _ = entry(jnp.minimum(index, total - 1))

        def item(n):
            return points_ref[pl.ds(pl.multiple_of(n * SLOTS + begin, GROUP), GROUP), :]

        cell = item(6).astype(jnp.int32) - 1
        plane = cell >> 16
        base_x = (((cell >> 8) & 255) - 1) & 255
        base_y = ((cell & 255) - 1) & 255
        taps = []
        for c in range(3):
            angle = item(3 + c) * (0.5 * math.pi)
            cosine, sine = 0.25 * jnp.cos(angle), 0.25 * jnp.sin(angle)
            taps.append([0.25 - sine, 0.25 + cosine, 0.25 + sine, 0.25 - cosine])
        scaled = []
        for weight_z in weigh(plane, taps[2]):
            scaled += [item(c) * weight_z for c in range(3)]
        high_x = (base_x >> 4).astype(F32)
        high_y = (base_y >> 4).astype(F32)
        zero = jnp.zeros((16, 128), BF16)

        def slice_of(r):
            lanes = pl.ds(r * 128, 128)

            def at(value):
                return jnp.broadcast_to(value[r : r + 1], (16, 128))

            near_x = windows(at(base_x), [at(t) for t in taps[0]])
            near_y = [p.astype(BF16) for p in windows(at(base_y), [at(t) for t in taps[1]])]
            left = [[(at(s) * piece).astype(BF16) for piece in near_x] for s in scaled]
            block_x = at(high_x).astype(BF16)
            block_y = at(high_y).astype(BF16)
            is_x = [block_x == jnp.asarray(g, BF16) for g in range(16)]
            is_y = [block_y == jnp.asarray(g, BF16) for g in range(16)]
            for g in range(16):
                right_ref[16 * g : 16 * g + 16, lanes] = jnp.where(
                    is_y[g], near_y[0], jnp.where(is_y[g - 1], near_y[1], zero)
                )
            for k, g in enumerate(blocks):
                for n, (low, high) in enumerate(left):
                    left_ref[pl.ds(rows * n + 16 * k, 16), lanes] = jnp.where(
                        is_x[g], low, jnp.where(is_x[g - 1], high, zero)
                    )

        return slice_of

    height = 3 * rows * targets
    parts = max(1, (height + tall // 2) // tall)

    def product(index, left_ref, right_ref, n):
        first = 0 if targets == 2 else 3 * rows * entry(jnp.minimum(index, total - 1))[2]
        low = tall * n
        high = height if n == parts - 1 else low + tall
        add(
            low if targets == 2 else pl.multiple_of(first + low, 8),
            high - low,
            lax.dot_general(
                left_ref[low:high], right_ref[...], NT, preferred_element_type=F32
            ),
        )

    (left_0, right_0), (left_1, right_1) = buffers

    def both(left_a, right_a, index, left_b, right_b):
        slice_of = build(index, left_b, right_b)
        done = 0
        for n in range(parts):
            product(index - 1, left_a, right_a, n)
            while done * parts < (n + 1) * GROUP and done < GROUP:
                slice_of(done)
                done += 1

    @pl.when(total > 0)
    def _():
        slice_of = build(0, left_0, right_0)
        for r in range(GROUP):
            slice_of(r)

        @pl.loop(0, total >> 1)
        def _(turn):
            both(left_0, right_0, 2 * turn + 1, left_1, right_1)
            both(left_1, right_1, 2 * turn + 2, left_0, right_0)

        @pl.when((total & 1) == 1)
        def _():
            for n in range(parts):
                product(total - 1, left_0, right_0, n)


def filled(points_ref, begin):
    code = points_ref[begin + 6 * SLOTS : begin + 7 * SLOTS, :]
    slot = iota(code.shape, 0).astype(F32)
    most = jnp.max(jnp.where((code > 0.5) & (code < 65536.5), slot + 1.0, 0.0))
    least = jnp.min(jnp.where(code > 65536.5, slot, float(SLOTS)))
    low = (most.astype(jnp.int32) + GROUP - 1) // GROUP
    return low, least.astype(jnp.int32) // GROUP


def weights_at(source, targets):
    def weigh(plane, taps):
        found = []
        for target in targets:
            pair = []
            for from_plane in range(2):
                reach = target - from_plane - 2 * source
                pair.append(taps[reach + 1] if -1 <= reach <= 2 else jnp.zeros_like(taps[0]))
            found.append(jnp.where(plane == 0, *pair))
        return found

    return weigh


def spread_own_points(own_ref, blocks, points_ref, buffers, add):
    points_ref[0 : 7 * SLOTS] = own_ref[...].T
    low, high = filled(points_ref, 0)
    high = jnp.maximum(low, high)

    def entry(index):
        step = jnp.where(index < low, index, high + index - low)
        return step * GROUP, weights_at(0, (0, 1)), 0

    total = low + SLOTS // GROUP - high
    spread_source(points_ref, 2, blocks, entry, total, buffers, add, 768)


def spread_near_points(below_ref, above_ref, blocks, points_ref, buffers, add):
    points_ref[0 : 7 * SLOTS] = below_ref[...].T
    points_ref[7 * SLOTS : 14 * SLOTS] = above_ref[...].T
    low, high = filled(points_ref, 0)
    low_above, _ = filled(points_ref, 7 * SLOTS)

    def entry(index):
        return (high + index) * GROUP, weights_at(-1, (0, 1)), 0

    spread_source(points_ref, 2, blocks, entry, SLOTS // GROUP - high, buffers, add)
    count = jnp.minimum(low, high)

    def entry_of_one(index):
        above = index >= count
        step = jnp.where(above, index - count, index)

        def weigh(plane, taps):
            return [jnp.where(plane == 0, jnp.where(above, taps[0], taps[3]), 0.0)]

        return (
            jnp.where(above, 7 * SLOTS, 0) + step * GROUP,
            weigh,
            jnp.where(above, 1, 0),
        )

    spread_source(points_ref, 1, blocks, entry_of_one, count + low_above, buffers, add)


def spread_scratch(blocks):
    return [pltpu.VMEM((14 * SLOTS, 128), F32)] + [
        pltpu.VMEM((96 * len(blocks), 128 * GROUP), BF16),
        pltpu.VMEM((256, 128 * GROUP), BF16),
    ] * 2


def spread_own_kernel(own_ref, field_ref, points_ref, left_0, right_0, left_1, right_1):
    field_ref[...] = jnp.zeros_like(field_ref)

    def add(first, count, value):
        field_ref[pl.ds(first, count)] += value

    buffers = ((left_0, right_0), (left_1, right_1))
    spread_own_points(own_ref, EVERY, points_ref, buffers, add)


def spread_own(own):
    return pl.pallas_call(
        spread_own_kernel,
        out_shape=jax.ShapeDtypeStruct((6 * WIDTH, WIDTH), F32),
        in_specs=[VMEM],
        out_specs=VMEM,
        scratch_shapes=spread_scratch(EVERY),
        compiler_params=params(14),
        cost_estimate=cost(8),
        name="spread_own",
    )(own)


def signed(item, vector):
    total = None
    for sign, value in zip((velocity_x[item], velocity_y[item], velocity_z[item]), vector):
        if sign:
            value = value if sign > 0 else -value
            total = value if total is None else total + value
    return total


def post_collision(current, push):
    density = current[0]
    for item in range(1, 19):
        density = density + current[item]
    moment = []
    for table in (velocity_x, velocity_y, velocity_z):
        plus = [current[i] for i in range(19) if table[i] > 0]
        minus = [current[i] for i in range(19) if table[i] < 0]
        moment.append(functools.reduce(jnp.add, plus) - functools.reduce(jnp.add, minus))
    inverse = 1.0 / density
    rate = 1.0 / relax_time
    half = 1.0 - 0.5 * rate
    flux = [m + 0.5 * f for m, f in zip(moment, push)]
    flow = [j * inverse for j in flux]
    rest = rate * density
    for u, j, f in zip(flow, flux, push):
        rest = rest - u * ((1.5 * rate) * j + (3.0 * half) * f)
    linear = [(3.0 * rate) * j + (3.0 * half) * f for j, f in zip(flux, push)]
    square = [(4.5 * rate) * j + (9.0 * half) * f for j, f in zip(flux, push)]
    result = [None] * 19
    result[10] = (1.0 - rate) * current[10] + (1.0 / 3) * rest
    for one, other in pairs:
        weight = 1.0 / 18 if one in (0, 11, 13) else 1.0 / 36
        even = weight * (rest + signed(one, flow) * signed(one, square))
        odd = weight * signed(one, linear)
        result[one] = (1.0 - rate) * current[one] + (even + odd)
        result[other] = (1.0 - rate) * current[other] + (even - odd)
    return result


def row_loads(start, rows, moves, sem):
    spans = [(start - 8, rows + 16, 0)]
    if start == 0:
        spans = [(WIDTH - 8, 8, 0), (0, rows + 8, 8)]
    elif start + rows == WIDTH:
        spans = [(start - 8, rows + 8, 0), (0, 8, rows + 8)]
    loads = []
    for z in range(2):
        group = []
        for n, (source, target) in enumerate(moves):
            for k, (first, count, place) in enumerate(spans):
                group.append(
                    pltpu.make_async_copy(
                        source.at[z, :, pl.ds(first, count)],
                        target.at[z, :, pl.ds(place, count)],
                        sem.at[z, n, k],
                    )
                )
        loads.append(group)
    for copy in loads[0] + loads[1]:
        copy.start()
    return loads


def collide_rows(
    start, rows, loads, current_ref, push_of, moved_ref, up_ref, down_ref, out_ref, carry_ref, out_sem
):
    stores = []
    row = iota((8, WIDTH), 0)
    for z in range(2):
        for copy in loads[z]:
            copy.wait()

        @pl.loop(0, rows // 8 + 2, unroll=9)
        def _(step):
            here = pl.multiple_of(step * 8, 8)
            now = pl.multiple_of(step * 8 + 8, 8)
            current = [current_ref[z, i, pl.ds(here, 8), :] for i in range(19)]
            result = post_collision(current, push_of(z, step))
            slot = 0
            for i in range(19):
                value = result[i]
                if velocity_y[i]:
                    value = pltpu.roll(value, velocity_y[i] % WIDTH, 1)
                if velocity_x[i] == 0:
                    out_ref[z, i, pl.ds(now, 8), :] = value
                    continue
                value = pltpu.roll(value, velocity_x[i] % 8, 0)
                old = carry_ref[slot]
                carry_ref[slot] = value
                slot += 1
                if velocity_x[i] > 0:
                    out_ref[z, i, pl.ds(now, 8), :] = jnp.where(row == 0, old, value)
                else:
                    out_ref[z, i, pl.ds(here, 8), :] = jnp.where(row == 7, value, old)

        within = pl.ds(start, rows)
        for n, (low, high, place) in enumerate(
            (
                (0, 5, moved_ref.at[1, 0:5, within] if z == 0 else up_ref),
                (5, 10, moved_ref.at[0, 5:10, within] if z == 1 else down_ref),
                (10, 19, moved_ref.at[z, 10:19, within]),
            )
        ):
            copy = pltpu.make_async_copy(
                out_ref.at[z, low:high, pl.ds(16, rows)], place, out_sem.at[z, n]
            )
            copy.start()
            stores.append(copy)
    for copy in stores:
        copy.wait()


def collide_scratch(rows):
    return [
        pltpu.VMEM((2, 19, rows + 16, WIDTH), F32),
        pltpu.VMEM((2, 19, rows + 24, WIDTH), F32),
        pltpu.VMEM((10, 8, WIDTH), F32),
        pltpu.SemaphoreType.DMA((2, 2, 2)),
        pltpu.SemaphoreType.DMA((2, 3)),
    ]


def collide_shapes(rows):
    return (
        jax.ShapeDtypeStruct((2, 19, WIDTH, WIDTH), F32),
        jax.ShapeDtypeStruct((5, rows, WIDTH), F32),
        jax.ShapeDtypeStruct((5, rows, WIDTH), F32),
    )


def collide_kernel(
    start,
    rows,
    populations_ref,
    field_ref,
    held_ref,
    moved_ref,
    up_ref,
    down_ref,
    push_ref,
    current_ref,
    out_ref,
    carry_ref,
    in_sem,
    out_sem,
):
    loads = row_loads(
        start, rows, ((populations_ref, current_ref), (field_ref, push_ref)), in_sem
    )

    def push_of(z, step):
        return [push_ref[z, c, pl.ds(pl.multiple_of(step * 8, 8), 8), :] for c in range(3)]

    collide_rows(
        start,
        rows,
        loads,
        current_ref,
        push_of,
        moved_ref,
        up_ref,
        down_ref,
        out_ref,
        carry_ref,
        out_sem,
    )


def collide(start, rows, populations, field, held):
    return pl.pallas_call(
        functools.partial(collide_kernel, start, rows),
        out_shape=collide_shapes(rows),
        in_specs=[HBM, HBM, ANY],
        out_specs=(ANY, VMEM, VMEM),
        scratch_shapes=[pltpu.VMEM((2, 3, rows + 16, WIDTH), F32)] + collide_scratch(rows),
        input_output_aliases={2: 0},
        compiler_params=params(50),
        cost_estimate=cost(9),
        name="collide",
    )(populations, field, held)


def spread_near_kernel(
    rows,
    below_ref,
    above_ref,
    held_ref,
    populations_ref,
    field_to,
    moved_ref,
    up_ref,
    down_ref,
    field_ref,
    points_ref,
    left_0,
    right_0,
    left_1,
    right_1,
    field_sem,
    current_ref,
    out_ref,
    carry_ref,
    in_sem,
    out_sem,
):
    loads = row_loads(0, rows, ((populations_ref, current_ref),), in_sem)

    def add(first, count, value):
        field_ref[pl.ds(first, count)] += value

    buffers = ((left_0, right_0), (left_1, right_1))
    field_ref[...] = held_ref[...]
    spread_near_points(below_ref, above_ref, EVERY, points_ref, buffers, add)
    store = pltpu.make_async_copy(field_ref, field_to, field_sem)
    store.start()

    def push_of(z, step):
        place = (step * 8 + WIDTH - 8) & (WIDTH - 1)
        return [
            field_ref[pl.ds(pl.multiple_of((3 * z + c) * WIDTH + place, 8), 8), :]
            for c in range(3)
        ]

    collide_rows(
        0,
        rows,
        loads,
        current_ref,
        push_of,
        moved_ref,
        up_ref,
        down_ref,
        out_ref,
        carry_ref,
        out_sem,
    )
    store.wait()


def spread_near(rows, below, above, field, populations):
    return pl.pallas_call(
        functools.partial(spread_near_kernel, rows),
        out_shape=(jax.ShapeDtypeStruct((1536, WIDTH), F32),) + collide_shapes(rows),
        in_specs=[VMEM] * 3 + [HBM],
        out_specs=(HBM, ANY, VMEM, VMEM),
        scratch_shapes=[pltpu.VMEM((1536, WIDTH), F32)]
        + spread_scratch(EVERY)
        + [pltpu.SemaphoreType.DMA]
        + collide_scratch(rows),
        compiler_params=params(50),
        cost_estimate=cost(18),
        name="spread_near",
    )(below, above, field, populations)


def place_kernel(starts, *refs):
    count = len(starts)
    ups, downs = refs[:count], refs[count : 2 * count]
    moved_ref, sem = refs[2 * count + 1 :]
    copies = []
    for n, start in enumerate(starts):
        within = pl.ds(start, ups[n].shape[1])
        copies += [
            pltpu.make_async_copy(ups[n], moved_ref.at[0, 0:5, within], sem.at[0, n]),
            pltpu.make_async_copy(downs[n], moved_ref.at[1, 5:10, within], sem.at[1, n]),
        ]
    for copy in copies:
        copy.start()
    for copy in copies:
        copy.wait()


def place(starts, ups, downs, moved):
    count = len(starts)
    return pl.pallas_call(
        functools.partial(place_kernel, starts),
        out_shape=jax.ShapeDtypeStruct(moved.shape, F32),
        in_specs=[VMEM] * (2 * count) + [ANY],
        out_specs=ANY,
        scratch_shapes=[pltpu.SemaphoreType.DMA((2, count))],
        input_output_aliases={2 * count: 0},
        compiler_params=params(8),
        cost_estimate=cost(1),
        name="place",
    )(*ups, *downs, moved)


def passed_along(value, steps, axis=("ves", "shard"), wrap=True):
    count = math.prod(lax.axis_size(a) for a in axis)
    return lax.ppermute(
        value,
        axis,
        [(i, (i + steps) % count) for i in range(count) if wrap or 0 <= i + steps < count],
    )


def cost(microseconds):
    return pl.CostEstimate(
        flops=microseconds * 10**9, bytes_accessed=microseconds * 10**6, transcendentals=0
    )


def params(megabytes):
    return pltpu.CompilerParams(vmem_limit_bytes=megabytes * 1024 * 1024)


def on_device(displacement, tension, bending, offset, owner, cell, populations):
    shape = jax.ShapeDtypeStruct
    before = passed_along(displacement[:, :, -2:], 1, ("shard",), False)
    after = passed_along(displacement[:, :, :2], -1, ("shard",), False)
    owner_rows = owner.reshape(32, 128)
    cell_rows = cell.reshape(32, 128)
    slot = pl.pallas_call(
        rank_kernel,
        out_shape=shape((32, 128), jnp.int32),
        in_specs=[HBM] * 2,
        out_specs=VMEM,
        scratch_shapes=[
            pltpu.VMEM((32, 128), jnp.int32),
            pltpu.VMEM((32, 128), jnp.int32),
            pltpu.SemaphoreType.DMA((2,)),
        ],
        compiler_params=params(60),
        cost_estimate=cost(3),
        name="rank",
    )(owner_rows, cell_rows)
    membrane_force, send = pl.pallas_call(
        pack_kernel,
        out_shape=(shape((3, 2, 16, 128), F32), shape((DEVICES, 1, 7 * SLOTS), F32)),
        in_specs=[HBM] * 3 + [VMEM] * 2 + [HBM] * 3 + [VMEM],
        out_specs=(VMEM, VMEM),
        scratch_shapes=[
            pltpu.SMEM((2,), F32),
            pltpu.SMEM((2,), F32),
            pltpu.VMEM((3, 2, 16, 128), F32),
            pltpu.VMEM((32, 128), jnp.int32),
            pltpu.VMEM((32, 128), jnp.int32),
            pltpu.VMEM((3, 2, 32, 128), F32),
            pltpu.VMEM((3, 2, 32, 128), F32),
            pltpu.VMEM((15 * SLOTS, 4096), BF16),
            pltpu.VMEM((DEVICES, 4096), BF16),
            pltpu.SemaphoreType.DMA((6,)),
        ],
        compiler_params=params(60),
        cost_estimate=cost(5),
        name="pack",
    )(
        tension, bending, displacement, before, after, offset, owner_rows, cell_rows, slot
    )
    own = lax.all_to_all(send, ("ves", "shard"), split_axis=0, concat_axis=0, tiled=True)
    own = own.reshape(DEVICES, 7 * SLOTS)
    below = passed_along(own, 1)
    above = passed_along(own, -1)
    start = CHUNKS[0]
    field, moved, up, down = spread_near(start, below, above, spread_own(own), populations)
    force_field = field.reshape(2, 3, WIDTH, WIDTH)
    ups, downs, starts = [passed_along(up, 1)], [passed_along(down, -1)], [0]
    for rows in CHUNKS[1:]:
        moved, up, down = collide(start, rows, populations, force_field, moved)
        ups.append(passed_along(up, 1))
        downs.append(passed_along(down, -1))
        starts.append(start)
        start += rows
    moved = place(starts[:-1], ups[:-1], downs[:-1], moved)
    moved = place(starts[-1:], ups[-1:], downs[-1:], moved)
    return (membrane_force, force_field, moved)


def solution(mesh):
    return jax.shard_map(
        on_device,
        mesh=mesh,
        in_specs=(
            P(None, "ves", "shard", None),
            P("ves"),
            P("ves"),
            P(None, "ves", "shard", None),
            P("ves", "shard", None),
            P("ves", "shard", None),
            P(("ves", "shard"), None, None, None),
        ),
        out_specs=(
            P(None, "ves", "shard", None),
            P(("ves", "shard"), None, None, None),
            P(("ves", "shard"), None, None, None),
        ),
        check_vma=False,
    )
```
